256 devices in a mesh: chan: 128 (over z, y_lo, x, core), freq: 2 (over y_hi).
Axes of the slice: x: 4, y: 4 (y_hi: 2, y_lo: 2; y = y_hi * 2 + y_lo), z: 8, core: 2. Of those that a mesh axis runs over, the one named last changes fastest.
Arguments:
- spectra: bfloat16 [2, 8, 4096, 1024], P(None, None, 'chan', 'freq'), may hold values from -60 to 60
- seg_mask: int32 [4096, 8], P('chan'), may hold values 0 or 1
Outputs:
- correlations: bfloat16 [2, 256, 4096, 512], P('freq', None, 'chan')
The draws below stay inside these ranges and needn't reach their ends.
All inputs are finite; a program needn't handle non-finite values. No bound on the sum of `seg_mask` on one device may be relied on, other than what follows from the above.
Results may differ from the reference program's by a relative error of at most 0.017.
Values may be sent and summed in bfloat16 or wider, within the bound.
No kernel may reach another device: no remote copies, remote signals or barrier semaphores. Data moves between devices by JAX's collectives and lax.ppermute only.
A program may use at most 192 MiB of HBM per device.

```python
import math
import jax
import jax.numpy as jnp
from jax import lax

CH_DEV = 32
BAND = 512
FBINS = 1024
SEGMENTS = 8
HALF = 64
LAGS = 256
NFFT = 2048
CHANNELS = 4096
FGROUP = 512
N_FREQ = 2


def draw_spectra(key, part):
    key = jax.random.fold_in(key, 11)
    base_key, scale_key = jax.random.split(key, 2)
    shape = (2, SEGMENTS, CHANNELS, FBINS)
    channel_scale = jnp.exp(jax.random.uniform(scale_key, (CHANNELS,), jnp.float32) * jnp.log(10.0))
    values = jnp.clip(jax.random.normal(base_key, shape, jnp.float32), -6.0, 6.0)
    return (values * channel_scale[None, None, :, None]).astype(jnp.bfloat16)


def touch_ends(result, own_key, smallest, top_value):
    shape = result.shape
    place = [jax.random.randint(jax.random.fold_in(own_key, axis), (), 0, shape[axis]) for axis in range(len(shape))]
    result = result.at[tuple(place)].set(smallest)
    longest = shape.index(max(shape))
    place[longest] = (place[longest] + 1) % shape[longest]
    return result.at[tuple(place)].set(top_value)


def setup_inputs(seed: int = 0) -> dict:
    seeds = jax.random.split(jax.random.key(seed), 3)
    return {
        "spectra": draw_spectra(jax.random.fold_in(seeds[2], 71), 0),
        "seg_mask": touch_ends((jax.random.randint(seeds[1], (CHANNELS, SEGMENTS), 0, 4) < 3).astype(jnp.int32), jax.random.fold_in(seeds[1], 1), 0, 1),
    }


EPSILON = 1e-06

def band_rows(matrix, band):
    leading = matrix.shape[:-2]
    height = matrix.shape[-2]
    breadth = matrix.shape[-1]
    flattened = matrix.reshape(leading + (height * breadth,))
    padded = jnp.pad(flattened, [(0, 0)] * len(leading) + [(0, height)])
    return padded.reshape(leading + (height, breadth + 1))[..., :band]

def lag_weights(lag_row, first_bin, bin_count, lag_count):
    freq_index = first_bin + jnp.arange(bin_count, dtype=jnp.int32)
    lag_index = jnp.arange(lag_count, dtype=jnp.int32)
    cycles = lag_index[:, None] * freq_index[None, :] % NFFT
    angles = cycles.astype(jnp.float32) * (2.0 * math.pi / NFFT)
    values = jnp.where(lag_row == 0, jnp.cos(angles), -jnp.sin(angles)) * FBINS ** (-0.5)
    return values.astype(jnp.bfloat16)

def reference(spectra, seg_mask):
    spectral = spectra.astype(jnp.float32)
    magnitude = jnp.sqrt(spectral[0] * spectral[0] + spectral[1] * spectral[1])
    summed = lax.reduce_window(magnitude, jnp.zeros((), magnitude.dtype), lax.add, (1, 1, 2 * HALF + 1), (1, 1, 1), ((0, 0), (0, 0), (HALF, HALF)))
    global_bin = jnp.arange(FBINS, dtype=jnp.int32)
    counted = (jnp.minimum(global_bin + HALF, FBINS - 1) - jnp.maximum(global_bin - HALF, 0) + 1).astype(jnp.float32)
    levels = summed / counted + EPSILON
    validity = seg_mask.astype(jnp.float32)
    whitened = (spectral / levels[None] * validity.T[None, :, :, None]).astype(jnp.bfloat16)
    padded = jnp.pad(whitened, ((0, 0), (0, 0), (0, BAND), (0, 0)))
    padded_valid = jnp.pad(validity, ((0, BAND), (0, 0)))
    flipped = jnp.stack([padded[1], -padded[0]])
    tables = [lag_weights(0, 0, FBINS, LAGS).astype(jnp.float32), lag_weights(1, 0, FBINS, LAGS).astype(jnp.float32)]

    def one_block(block_index):
        begin = (block_index * CH_DEV).astype(jnp.int32)
        source = lax.dynamic_slice_in_dim(padded, begin, CH_DEV, 2).astype(jnp.float32)
        partners = [lax.dynamic_slice_in_dim(padded, begin, CH_DEV + BAND, 2).astype(jnp.float32), lax.dynamic_slice_in_dim(flipped, begin, CH_DEV + BAND, 2).astype(jnp.float32)]
        valid_own = lax.dynamic_slice_in_dim(padded_valid, begin, CH_DEV, 0)
        valid_band = lax.dynamic_slice_in_dim(padded_valid, begin, CH_DEV + BAND, 0)
        pair_count = band_rows(jnp.dot(valid_own, valid_band.T, precision=lax.Precision.HIGHEST), BAND)
        inverse = 1.0 / jnp.maximum(pair_count, 1.0)
        results = []
        for lag_row in (0, 1):
            product = jnp.einsum('ksCf,ksWf->fCW', source, partners[lag_row], precision=lax.Precision.HIGHEST)
            spectrum = (band_rows(product, BAND) * inverse).astype(jnp.bfloat16).astype(jnp.float32)
            running = jnp.zeros((LAGS, CH_DEV * BAND), jnp.float32)
            for group in range(N_FREQ):
                group_start = group * FGROUP
                partial_sum = jnp.dot(tables[lag_row][:, group_start:group_start + FGROUP], spectrum[group_start:group_start + FGROUP].reshape(FGROUP, CH_DEV * BAND), precision=lax.Precision.HIGHEST)
                running = running + lax.optimization_barrier(partial_sum.astype(jnp.bfloat16)).astype(jnp.float32)
            results.append(running.astype(jnp.bfloat16).reshape(LAGS, CH_DEV, BAND))
        return jnp.stack(results)
    blocks = lax.map(one_block, jnp.arange(CHANNELS // CH_DEV, dtype=jnp.int32))
    return jnp.transpose(blocks, (1, 2, 0, 3, 4)).reshape(2, LAGS, CHANNELS, BAND)
```

```python
import math

import jax
import jax.numpy as jnp
import ml_dtypes
import numpy as np
from jax import lax
from jax.experimental import pallas as pl
from jax.experimental.pallas import tpu as pltpu
from jax.sharding import PartitionSpec as P

BAND = 512
FBINS = 1024
HALF = 64
LAGS = 256
NFFT = 2048
EPSILON = 1e-06
SEGMENTS = 8
CH = 32
BINS = 512
GROUP = 16
GROUPS = BINS // GROUP
DEPTH = 2 * SEGMENTS * GROUP
STEP = 4
ROWS = 2
LINE = 4
CSTEP = 4
AXES = ("chan", "freq")
VMEM = 60 * 1024 * 1024
INTERPRET = False


def moved(value, back=(0, 0, 0), core=0, freq=0):
    count, halves = lax.axis_size("chan"), lax.axis_size("freq")
    planes = count // (ROWS * LINE * 2)
    pairs = []
    for index in range(count * halves):
        rest, f = divmod(index, halves)
        rest, k = divmod(rest, 2)
        rest, x = divmod(rest, LINE)
        z, y = divmod(rest, ROWS)
        z, y, x = (z - back[0]) % planes, (y - back[1]) % ROWS, (x - back[2]) % LINE
        pairs.append((index, (((z * ROWS + y) * LINE + x) * 2 + (k ^ core)) * halves + (f ^ freq)))
    return lax.ppermute(value, AXES, pairs)


def whiten_kernel(rank_ref, spectra_ref, rim_ref, mask_ref, out_ref):
    rank = rank_ref[0]
    real = spectra_ref[0].astype(jnp.float32)
    imag = spectra_ref[1].astype(jnp.float32)
    magnitude = jnp.sqrt(real * real + imag * imag).reshape(SEGMENTS * CH, BINS)
    rim_real = rim_ref[0].astype(jnp.float32)
    rim_imag = rim_ref[1].astype(jnp.float32)
    rim = jnp.sqrt(rim_real * rim_real + rim_imag * rim_imag).reshape(SEGMENTS * CH, 128)

    def window_sum(values, positions):
        target = lax.broadcasted_iota(jnp.int32, (values.shape[1], BINS), 1)
        near = jnp.abs(positions - target) <= HALF
        table = jnp.where(near, 1.0, 0.0).astype(jnp.bfloat16)
        high = values.astype(jnp.bfloat16)
        low = (values - high.astype(jnp.float32)).astype(jnp.bfloat16)
        return jnp.dot(high, table, preferred_element_type=jnp.float32) + jnp.dot(
            low, table, preferred_element_type=jnp.float32
        )

    inner = lax.broadcasted_iota(jnp.int32, (BINS, BINS), 0)
    outer = lax.broadcasted_iota(jnp.int32, (128, BINS), 0) + jnp.where(rank == 0, BINS, -128)
    summed = window_sum(magnitude, inner) + window_sum(rim, outer)
    bin_index = rank * BINS + lax.broadcasted_iota(jnp.int32, (1, BINS), 1)
    counted = (
        jnp.minimum(bin_index + HALF, FBINS - 1) - jnp.maximum(bin_index - HALF, 0) + 1
    ).astype(jnp.float32)
    levels = summed / counted + EPSILON
    scale = (1.0 / levels).reshape(SEGMENTS, CH, BINS)
    valid = mask_ref[...].astype(jnp.float32)
    out_ref[GROUPS] = jnp.concatenate(
        [valid, jnp.zeros((CH, DEPTH - SEGMENTS), jnp.float32)], 1
    ).astype(jnp.bfloat16)
    lane = lax.broadcasted_iota(jnp.int32, (CH, 128), 1)
    for p, part in enumerate((real, imag)):
        for tile in range(BINS // 128):
            cut = slice(tile * 128, tile * 128 + 128)
            rows = [
                part[s, :, cut] * scale[s, :, cut] * valid[:, s : s + 1] for s in range(SEGMENTS)
            ]
            for bit in (1, 2, 4):
                upper = (lane // GROUP) & bit != 0
                for i in range(SEGMENTS):
                    if i & bit:
                        continue
                    a, b = rows[i], rows[i + bit]
                    rows[i] = jnp.where(upper, pltpu.roll(b, bit * GROUP, 1), a)
                    rows[i + bit] = jnp.where(upper, b, pltpu.roll(a, 128 - bit * GROUP, 1))
            for g in range(SEGMENTS):
                out_ref[tile * SEGMENTS + g, :, p * 128 : p * 128 + 128] = rows[g].astype(
                    jnp.bfloat16
                )


def whiten(rank, spectra, rim, mask):
    return pl.pallas_call(
        whiten_kernel,
        out_shape=jax.ShapeDtypeStruct((GROUPS + 1, CH, DEPTH), jnp.bfloat16),
        in_specs=[pl.BlockSpec(memory_space=pltpu.SMEM)]
        + [pl.BlockSpec(memory_space=pltpu.VMEM)] * 3,
        out_specs=pl.BlockSpec(memory_space=pltpu.VMEM),
        compiler_params=pltpu.CompilerParams(vmem_limit_bytes=VMEM),
        name="whiten",
    )(rank, spectra, rim, mask)


def piece_kernel(steps, units, final, place_ref, *refs):
    arrays = sorted({unit[0] for unit in units.values()})
    own_ref, source_refs, refs = refs[0], refs[1:3], refs[3:]
    array_refs = dict(zip(arrays, refs[: len(arrays)]))
    table_ref, refs = refs[len(arrays)], refs[len(arrays) + 1 :]
    closing = 0 in steps
    earlier = [j for j in range(LINE) if j not in steps] if final else []
    earlier_refs, refs = refs[: len(earlier)], refs[len(earlier) :]
    if final:
        result_ref, refs = refs[-1], refs[:-1]
    out_ref, rows_ref, flags_ref, diagonal_ref, product_ref, inverse_ref, weights_ref, sems = refs
    core, x, chip, chips = place_ref[0], place_ref[1], place_ref[2], place_ref[3]
    rank = place_ref[4]
    step = pl.program_id(0)
    width = 128 * len(steps)
    blocks = 8 * len(steps) + 4 * closing
    corr_steps = GROUPS // STEP

    def unit_at(j, kind, half, layer):
        if isinstance(kind, int) and kind == 2:
            return blocks - 4 + 2 * half + layer
        return ((steps.index(j) * 2 + kind) * 2 + half) * 2 + layer

    def columns(load):
        listed = []
        for j in steps:
            wraps = jnp.where(x + j >= LINE, 1, 0)
            for upper in (wraps, 1 - wraps):
                for layer in (core, 1 - core):
                    listed.append(load(j, upper, layer))
        if closing:
            listed += [load(0, 2, core), load(0, 2, 1 - core)]
        return jnp.concatenate(listed, 0)

    def fetch(number):
        slot = number % 2
        for key, (name, index) in units.items():
            pltpu.make_async_copy(
                array_refs[name].at[index, pl.ds(number * STEP, STEP)],
                rows_ref.at[slot, unit_at(*key)],
                sems.at[slot],
            ).start()

    @pl.when(step == 0)
    def begin():
        fetch(0)
        pltpu.make_async_copy(table_ref.at[rank], weights_ref, sems.at[3]).start()
        for (j, kind, half, layer), (name, index) in units.items():
            if half == 0:
                pltpu.make_async_copy(
                    array_refs[name].at[index, GROUPS],
                    flags_ref.at[unit_at(j, kind, 0, layer) // 4 * 2 + layer],
                    sems.at[2],
                ).start()
        pltpu.make_async_copy(flags_ref, flags_ref, sems.at[2]).wait()
        counts = lax.dot_general(
            own_ref[0],
            columns(lambda j, kind, layer: flags_ref[unit_at(j, kind, 0, layer) // 4 * 2 + layer]),
            (((1,), (1,)), ((), ())),
            preferred_element_type=jnp.float32,
        )
        inverse = 1.0 / jnp.maximum(counts, 1.0)
        column = lax.broadcasted_iota(jnp.int32, (CH, 64), 1)
        channel = lax.broadcasted_iota(jnp.int32, (CH, 64), 0)
        parts = []
        for n in range(2 * len(steps)):
            offset = steps[n // 2] + 4 * (n % 2)
            part = jnp.where(chip + offset < chips, inverse[:, 64 * n : 64 * n + 64], 0.0)
            if offset == 0:
                after = jnp.where(chip + 8 < chips, inverse[:, width : width + 64], 0.0)
                part = jnp.where(column >= 32 * core + channel, part, after)
            parts.append(part)
        whole = jnp.concatenate(parts, 1)
        for c in range(CH):
            inverse_ref[c] = whole[c : c + 1]

    @pl.when(step < corr_steps)
    def correlate():
        @pl.when(step + 1 < corr_steps)
        def ahead():
            fetch(step + 1)

        slot = step % 2
        pltpu.make_async_copy(rows_ref.at[slot], rows_ref.at[slot], sems.at[slot]).wait()
        lane_bin = lax.broadcasted_iota(jnp.int32, (GROUP, DEPTH), 1) % GROUP
        own_bin = lane_bin == lax.broadcasted_iota(jnp.int32, (GROUP, DEPTH), 0)
        column = lax.broadcasted_iota(jnp.int32, (GROUP, 128), 1)

        def one_group(index, carry):
            for half in range(2):
                source = source_refs[half][index].astype(jnp.float32)
                real, imag = source[:, : DEPTH // 2], source[:, DEPTH // 2 :]
                source = jnp.concatenate(
                    [jnp.where(rank == 0, real, -imag), jnp.where(rank == 0, imag, real)], 1
                )
                for c in range(CH):
                    spread = jnp.broadcast_to(source[c : c + 1, :], (GROUP, DEPTH))
                    diagonal_ref[half, c * GROUP : (c + 1) * GROUP, :] = jnp.where(
                        own_bin, spread, 0.0
                    ).astype(jnp.bfloat16)
                product = lax.dot_general(
                    diagonal_ref[half],
                    columns(
                        lambda j, kind, layer: rows_ref[
                            slot, unit_at(j, kind, half, layer), index
                        ]
                    ),
                    (((1,), (1,)), ((), ())),
                    preferred_element_type=jnp.float32,
                )
                first_bin = pl.multiple_of(half * BINS + (step * STEP + index) * GROUP, GROUP)
                for c in range(CH):
                    part = product[c * GROUP : (c + 1) * GROUP]
                    here = pl.ds(c * FBINS + first_bin, GROUP)
                    if closing:
                        at = width - 128
                        tail = jnp.concatenate(
                            [part[:, width : width + 64], part[:, 64:128]], 1
                        )
                        head = jnp.where(column >= 32 * core + c, part[:, :128], tail)
                        part = jnp.concatenate([head, part[:, 128:width]], 1) if at else head
                    product_ref[here, :] = part.astype(jnp.bfloat16)
            return carry

        lax.fori_loop(0, STEP, one_group, 0, unroll=4)

    @pl.when(step >= corr_steps)
    def transform():
        lag_step = step - corr_steps

        @pl.when(lag_step == 0)
        def table_there():
            pltpu.make_async_copy(table_ref.at[rank], weights_ref, sems.at[3]).wait()

        def one_channel(index, carry):
            c = lag_step * CSTEP + index
            lags = jnp.dot(
                weights_ref[...],
                product_ref[pl.ds(pl.multiple_of(c * FBINS, FBINS), FBINS), :],
                preferred_element_type=jnp.float32,
            )
            lags = lags * inverse_ref[c]
            if not final:
                for n in range(len(steps)):
                    out_ref[n, index] = lags[:, 128 * n : 128 * n + 128].astype(jnp.bfloat16)
                return carry
            tiles = {j: lags[:, 128 * n : 128 * n + 128] for n, j in enumerate(steps)}
            for n, j in enumerate(earlier):
                tiles[j] = earlier_refs[n][0, index].astype(jnp.float32)
            shift = 32 * core + c
            low = [pltpu.roll(tiles[j], (128 - shift) % 128, 1) for j in range(LINE)]
            high = [pltpu.roll(tiles[j], 64 - shift, 1) for j in range(LINE)]
            lane = lax.broadcasted_iota(jnp.int32, (LAGS, 128), 1)
            first, second = lane < 64 - shift, lane < 128 - shift
            slot = c % 16
            for u, (one, two, three) in enumerate(
                (
                    (low[0], high[1], low[2]),
                    (low[2], high[3], high[0]),
                    (high[0], low[1], high[2]),
                    (high[2], low[3], low[0]),
                )
            ):
                value = jnp.where(first, one, jnp.where(second, two, three))
                result_ref[u, pl.ds(pl.multiple_of(slot * LAGS, LAGS), LAGS), :] = value
            return carry

        lax.fori_loop(0, CSTEP, one_channel, 0, unroll=4)
        if final:

            @pl.when(lag_step % (16 // CSTEP) == 16 // CSTEP - 1)
            def flush():
                for u in range(4):

                    def some_lags(number, carry, u=u):
                        at = pl.multiple_of(number * 8, 8)
                        block = jnp.stack(
                            [result_ref[u, pl.ds(n * LAGS + at, 8), :] for n in range(16)]
                        )
                        out_ref[pl.ds(at, 8), :, u * 128 : u * 128 + 128] = jnp.swapaxes(
                            block, 0, 1
                        ).astype(jnp.bfloat16)
                        return carry

                    lax.fori_loop(0, LAGS // 8, some_lags, 0, unroll=4)


def piece(place, own, sources, steps, arrays, units, weights, earlier=None):
    final = earlier is not None
    width = 128 * len(steps)
    rows = width + 64 * (0 in steps)
    corr_steps = GROUPS // STEP
    lag_steps = CH // CSTEP
    names = sorted({unit[0] for unit in units.values()})

    def lag_at(i):
        return jnp.maximum(i - corr_steps, 0)

    source_spec = pl.BlockSpec((STEP, CH, DEPTH), lambda i: (jnp.minimum(i, corr_steps - 1), 0, 0))
    in_specs = [pl.BlockSpec(memory_space=pltpu.SMEM)]
    in_specs += [pl.BlockSpec((1, CH, DEPTH), lambda i: (GROUPS, 0, 0))]
    in_specs += [source_spec] * 2
    in_specs += [pl.BlockSpec(memory_space=pl.ANY)] * len(names)
    in_specs += [pl.BlockSpec(memory_space=pl.ANY)]
    scratch = [
        pltpu.VMEM((2, rows // 16, STEP, CH, DEPTH), jnp.bfloat16),
        pltpu.VMEM((rows // 32, CH, DEPTH), jnp.bfloat16),
        pltpu.VMEM((2, CH * GROUP, DEPTH), jnp.bfloat16),
        pltpu.VMEM((CH * FBINS, width), jnp.bfloat16),
        pltpu.VMEM((CH, 1, width), jnp.float32),
        pltpu.VMEM((LAGS, FBINS), jnp.bfloat16),
        pltpu.SemaphoreType.DMA((4,)),
    ]
    operands = [place, own, *sources, *(arrays[name] for name in names), weights]
    if final:
        for j in range(LINE):
            if j not in steps:
                array, index = earlier[j]
                operands.append(array)
                in_specs.append(
                    pl.BlockSpec(
                        (1, CSTEP, LAGS, 128), lambda i, index=index: (index, lag_at(i), 0, 0)
                    )
                )
        scratch += [pltpu.VMEM((4, LAGS * 16, 128), jnp.float32)]
        out_shape = jax.ShapeDtypeStruct((LAGS, CH, BAND), jnp.bfloat16)
        out_specs = pl.BlockSpec((LAGS, 16, BAND), lambda i: (0, lag_at(i) * CSTEP // 16, 0))
    else:
        out_shape = jax.ShapeDtypeStruct((len(steps), CH, LAGS, 128), jnp.bfloat16)
        out_specs = pl.BlockSpec((len(steps), CSTEP, LAGS, 128), lambda i: (0, lag_at(i), 0, 0))
    flops = 2 * CH * FBINS * rows * (DEPTH + LAGS)
    moved_bytes = 4 * rows * BINS * DEPTH // GROUP + 2 * CH * LAGS * width
    return pl.pallas_call(
        lambda *refs: piece_kernel(steps, units, final, *refs),
        grid=(corr_steps + lag_steps,),
        out_shape=out_shape,
        in_specs=in_specs,
        out_specs=out_specs,
        scratch_shapes=scratch,
        compiler_params=pltpu.CompilerParams(
            vmem_limit_bytes=VMEM, dimension_semantics=("arbitrary",)
        ),
        cost_estimate=pl.CostEstimate(flops=flops, bytes_accessed=moved_bytes, transcendentals=0),
        name="piece_" + "_".join(map(str, steps)),
    )(*operands)


def lag_table():
    lag_index = np.arange(LAGS, dtype=np.int64)
    tables = []
    for rank in range(2):
        freq_index = (np.arange(FBINS, dtype=np.int64) + rank * BINS) % FBINS
        angles = (lag_index[:, None] * freq_index[None, :] % NFFT) * (2.0 * math.pi / NFFT)
        values = -np.sin(angles) if rank else np.cos(angles)
        tables.append((values * FBINS ** (-0.5)).astype(np.float32).astype(ml_dtypes.bfloat16))
    return np.stack(tables)


BARRIERS = ()
PIECES = ((0, 1, 2, 3),)
SWAPS = "stack"


def held_back(number, *values):
    return lax.optimization_barrier(values) if number in BARRIERS else values


def local(spectra, seg_mask):
    chan = lax.axis_index("chan")
    rank = lax.axis_index("freq")
    core, x, row = chan % 2, chan // 2 % LINE, chan // (2 * LINE) % ROWS
    place = jnp.stack([core, x, chan // 2, jnp.int32(lax.axis_size("chan") // 2), rank]).astype(jnp.int32)
    edge = jnp.where(rank == 0, spectra[..., BINS - 128 :], spectra[..., :128])
    rim = moved(edge, freq=1)
    own = whiten(rank.astype(jnp.int32).reshape(1), spectra, rim, seg_mask)

    other = {}

    def swap(blocks):
        if SWAPS == "stack":
            both = moved(jnp.stack(list(blocks.values())), core=1)
            for n, key in enumerate(blocks):
                other[key] = (both, n)
        else:
            for key, block in blocks.items():
                other[key] = (moved(block, core=1)[None], 0)

    after = moved(own, (1, 0, 0))
    flip = moved(own, freq=1)
    own_, after, flip = held_back(0, own, after, flip)
    along = {j: moved(jnp.where(x >= j, own_, after), (0, 0, j)) for j in (1, 3, 2)}
    crossing = jnp.where(row == 1, own_, after)
    cross = {0: moved(crossing, (0, 1, 0))}
    cross_flip = {0: moved(crossing, (0, 1, 0), freq=1)}
    after_flip = moved(flip, (1, 0, 0))
    (along, cross, cross_flip, after_flip) = held_back(1, along, cross, cross_flip, after_flip)
    along[0] = own
    along_flip = {0: flip}
    swap(
        {
            (0, 0, 0): own,
            (0, 0, 1): flip,
            (0, 1, 0): cross[0],
            (0, 1, 1): cross_flip[0],
            (0, 2, 0): after,
            (0, 2, 1): after_flip,
        }
    )
    for j in (1, 3):
        cross[j] = moved(cross[0], (0, 0, j))
        cross_flip[j] = moved(cross_flip[0], (0, 0, j))
        along_flip[j] = moved(along[j], freq=1)
    kept = {key: array for key, (array, index) in other.items()}
    cross, cross_flip, along_flip, kept = held_back(2, cross, cross_flip, along_flip, kept)
    for key, array in kept.items():
        other[key] = (array, other[key][1])
    swap(
        {
            (j, kind, half): blocks[j]
            for j in (1, 3)
            for kind, half, blocks in (
                (0, 0, along),
                (0, 1, along_flip),
                (1, 0, cross),
                (1, 1, cross_flip),
            )
        }
    )
    cross[2] = moved(cross[1], (0, 0, 1))
    cross_flip[2] = moved(cross_flip[3], (0, 0, 3))
    along_flip[2] = moved(along[2], freq=1)
    swap(
        {
            (2, 0, 0): along[2],
            (2, 0, 1): along_flip[2],
            (2, 1, 0): cross[2],
            (2, 1, 1): cross_flip[2],
        }
    )
    weights = jnp.asarray(lag_table())
    sources = [own, flip]
    mine = {(0, 2, 0): after, (0, 2, 1): after_flip}
    for j in range(LINE):
        mine[j, 0, 0], mine[j, 0, 1] = along[j], along_flip[j]
        mine[j, 1, 0], mine[j, 1, 1] = cross[j], cross_flip[j]

    def part(steps, earlier=None):
        arrays, units, known = {}, {}, {}
        for key in mine:
            if key[0] not in steps:
                continue
            for layer, (array, index) in enumerate(((mine[key][None], 0), other[key])):
                name = known.setdefault(id(array) if layer else key, len(known))
                arrays[name] = array
                units[(*key, layer)] = (name, index)
        return piece(place, own, sources, steps, arrays, units, weights, earlier)

    earlier = {}
    for steps in PIECES[:-1]:
        array = part(steps)
        for n, j in enumerate(steps):
            earlier[j] = (array, n)
    return part(PIECES[-1], earlier)[None]


def solution(mesh):
    placed = (P(None, None, "chan", "freq"), P("chan", None))
    return jax.shard_map(
        local, mesh=mesh, in_specs=placed, out_specs=P("freq", None, "chan", None), check_vma=False
    )
```

```python
import math

import jax
import jax.numpy as jnp
import ml_dtypes
import numpy as np
from jax import lax
from jax.experimental import pallas as pl
from jax.experimental.pallas import tpu as pltpu
from jax.sharding import PartitionSpec as P

BAND = 512
FBINS = 1024
HALF = 64
LAGS = 256
NFFT = 2048
EPSILON = 1e-06
SEGMENTS = 8
CH = 32
BINS = 512
GROUP = 16
GROUPS = BINS // GROUP
DEPTH = 2 * SEGMENTS * GROUP
STEP = 8
UNROLL = 8
BATCH = 16
CHUNK = 16
ROWS = 2
LINE = 4
CSTEP = 4
AXES = ("chan", "freq")
VMEM = 60 * 1024 * 1024
INTERPRET = False


def moved(value, back=(0, 0, 0), core=0, freq=0):
    count, halves = lax.axis_size("chan"), lax.axis_size("freq")
    planes = count // (ROWS * LINE * 2)
    pairs = []
    for index in range(count * halves):
        rest, f = divmod(index, halves)
        rest, k = divmod(rest, 2)
        rest, x = divmod(rest, LINE)
        z, y = divmod(rest, ROWS)
        z, y, x = (z - back[0]) % planes, (y - back[1]) % ROWS, (x - back[2]) % LINE
        pairs.append((index, (((z * ROWS + y) * LINE + x) * 2 + (k ^ core)) * halves + (f ^ freq)))
    return lax.ppermute(value, AXES, pairs)


def whiten_kernel(rank_ref, spectra_ref, rim_ref, mask_ref, out_ref):
    rank = rank_ref[0]
    real = spectra_ref[0].astype(jnp.float32)
    imag = spectra_ref[1].astype(jnp.float32)
    magnitude = jnp.sqrt(real * real + imag * imag).reshape(SEGMENTS * CH, BINS)
    rim_real = rim_ref[0].astype(jnp.float32)
    rim_imag = rim_ref[1].astype(jnp.float32)
    rim = jnp.sqrt(rim_real * rim_real + rim_imag * rim_imag).reshape(SEGMENTS * CH, 128)

    def window_sum(values, positions):
        target = lax.broadcasted_iota(jnp.int32, (values.shape[1], BINS), 1)
        near = jnp.abs(positions - target) <= HALF
        table = jnp.where(near, 1.0, 0.0).astype(jnp.bfloat16)
        high = values.astype(jnp.bfloat16)
        low = (values - high.astype(jnp.float32)).astype(jnp.bfloat16)
        return jnp.dot(high, table, preferred_element_type=jnp.float32) + jnp.dot(
            low, table, preferred_element_type=jnp.float32
        )

    inner = lax.broadcasted_iota(jnp.int32, (BINS, BINS), 0)
    outer = lax.broadcasted_iota(jnp.int32, (128, BINS), 0) + jnp.where(rank == 0, BINS, -128)
    summed = window_sum(magnitude, inner) + window_sum(rim, outer)
    bin_index = rank * BINS + lax.broadcasted_iota(jnp.int32, (1, BINS), 1)
    counted = (
        jnp.minimum(bin_index + HALF, FBINS - 1) - jnp.maximum(bin_index - HALF, 0) + 1
    ).astype(jnp.float32)
    levels = summed / counted + EPSILON
    scale = (1.0 / levels).reshape(SEGMENTS, CH, BINS)
    valid = mask_ref[...].astype(jnp.float32)
    out_ref[GROUPS] = jnp.concatenate(
        [valid, jnp.zeros((CH, DEPTH - SEGMENTS), jnp.float32)], 1
    ).astype(jnp.bfloat16)
    lane = lax.broadcasted_iota(jnp.int32, (CH, 128), 1)
    for p, part in enumerate((real, imag)):
        for tile in range(BINS // 128):
            cut = slice(tile * 128, tile * 128 + 128)
            rows = [
                part[s, :, cut] * scale[s, :, cut] * valid[:, s : s + 1] for s in range(SEGMENTS)
            ]
            for bit in (1, 2, 4):
                upper = (lane // GROUP) & bit != 0
                for i in range(SEGMENTS):
                    if i & bit:
                        continue
                    a, b = rows[i], rows[i + bit]
                    rows[i] = jnp.where(upper, pltpu.roll(b, bit * GROUP, 1), a)
                    rows[i + bit] = jnp.where(upper, b, pltpu.roll(a, 128 - bit * GROUP, 1))
            for g in range(SEGMENTS):
                out_ref[tile * SEGMENTS + g, :, p * 128 : p * 128 + 128] = rows[g].astype(
                    jnp.bfloat16
                )


def whiten(rank, spectra, rim, mask):
    return pl.pallas_call(
        whiten_kernel,
        out_shape=jax.ShapeDtypeStruct((GROUPS + 1, CH, DEPTH), jnp.bfloat16),
        in_specs=[pl.BlockSpec(memory_space=pltpu.SMEM)]
        + [pl.BlockSpec(memory_space=pltpu.VMEM)] * 3,
        out_specs=pl.BlockSpec(memory_space=pltpu.VMEM),
        compiler_params=pltpu.CompilerParams(vmem_limit_bytes=VMEM),
        name="whiten",
    )(rank, spectra, rim, mask)


def band_kernel(lies, place_ref, *refs):
    own_ref, source_refs, array_refs = refs[0], refs[1:3], refs[3 : 3 + len(lies)]
    (table_ref, out_ref, rows_ref, flags_ref, diagonal_ref, product_ref, inverse_ref) = refs[
        3 + len(lies) : 10 + len(lies)
    ]
    weights_ref, result_ref, staging_ref, sems, out_sems = refs[10 + len(lies) :]
    core, x, chip, chips, rank = [place_ref[n] for n in range(5)]
    step = pl.program_id(0)
    corr_steps = GROUPS // STEP
    place = {}
    count = 0
    spans = []
    for names in lies:
        spans.append((count, len(names)))
        for name in names:
            place[name] = count
            count += 1

    def order(half):
        listed = []

        def add(kinds, layer):
            listed.append(jnp.where(layer == 0, place[(*kinds, 0)], place[(*kinds, 1)]))

        for j in range(LINE):
            wraps = x + j >= LINE
            for upper in (0, 1):
                for layer in (core, 1 - core):
                    straight = [place[j, upper, half, n] for n in range(2)]
                    turned = [place[j, 1 - upper, half, n] for n in range(2)]
                    listed.append(
                        jnp.where(
                            wraps,
                            jnp.where(layer == 0, turned[0], turned[1]),
                            jnp.where(layer == 0, straight[0], straight[1]),
                        )
                    )
        for layer in (core, 1 - core):
            add((0, 2, half), layer)
        return listed

    def fetch(number):
        slot = number % 2
        for ref, (start, size) in zip(array_refs, spans):
            pltpu.make_async_copy(
                ref.at[:, pl.ds(number * STEP, STEP)],
                rows_ref.at[slot, pl.ds(start, size)],
                sems.at[slot],
            ).start()

    @pl.when(step == 0)
    def begin():
        fetch(0)
        pltpu.make_async_copy(table_ref.at[rank], weights_ref, sems.at[3]).start()
        for ref, (start, size) in zip(array_refs, spans):
            pltpu.make_async_copy(
                ref.at[:, GROUPS], flags_ref.at[pl.ds(start, size)], sems.at[2]
            ).start()

    @pl.when(step < corr_steps)
    def correlate():
        @pl.when(step + 1 < corr_steps)
        def ahead():
            fetch(step + 1)

        slot = step % 2
        pltpu.make_async_copy(rows_ref.at[slot], rows_ref.at[slot], sems.at[slot]).wait()
        lane_bin = lax.broadcasted_iota(jnp.int32, (GROUP, DEPTH), 1) % GROUP
        own_bin = lane_bin == lax.broadcasted_iota(jnp.int32, (GROUP, DEPTH), 0)
        column = lax.broadcasted_iota(jnp.int32, (GROUP, 128), 1)
        orders = [order(half) for half in range(2)]

        def one_group(index, carry):
            for half in range(2):
                source = source_refs[half][index].astype(jnp.float32)
                real, imag = source[:, : DEPTH // 2], source[:, DEPTH // 2 :]
                source = jnp.concatenate(
                    [jnp.where(rank == 0, real, -imag), jnp.where(rank == 0, imag, real)], 1
                )
                for c in range(CH):
                    spread = jnp.broadcast_to(source[c : c + 1, :], (GROUP, DEPTH))
                    diagonal_ref[half, c * GROUP : (c + 1) * GROUP, :] = jnp.where(
                        own_bin, spread, 0.0
                    ).astype(jnp.bfloat16)
                rows = jnp.concatenate([rows_ref[slot, at, index] for at in orders[half]], 0)
                product = lax.dot_general(
                    diagonal_ref[half],
                    rows,
                    (((1,), (1,)), ((), ())),
                    preferred_element_type=jnp.float32,
                )
                first_bin = pl.multiple_of(half * BINS + (step * STEP + index) * GROUP, GROUP)
                for c in range(CH):
                    part = product[c * GROUP : (c + 1) * GROUP]
                    here = pl.ds(c * FBINS + first_bin, GROUP)
                    tail = jnp.concatenate([part[:, BAND:], part[:, 64:128]], 1)
                    head = jnp.where(column >= 32 * core + c, part[:, :128], tail)
                    product_ref[here, :] = jnp.concatenate([head, part[:, 128:BAND]], 1).astype(
                        jnp.bfloat16
                    )
            return carry

        lax.fori_loop(0, STEP, one_group, 0, unroll=UNROLL)

    @pl.when(step == corr_steps)
    def scales():
        pltpu.make_async_copy(table_ref.at[rank], weights_ref, sems.at[3]).wait()
        pltpu.make_async_copy(flags_ref, flags_ref, sems.at[2]).wait()
        counts = lax.dot_general(
            own_ref[0],
            jnp.concatenate([flags_ref[at] for at in order(0)], 0),
            (((1,), (1,)), ((), ())),
            preferred_element_type=jnp.float32,
        )
        inverse = 1.0 / jnp.maximum(counts, 1.0)
        column = lax.broadcasted_iota(jnp.int32, (CH, 64), 1)
        channel = lax.broadcasted_iota(jnp.int32, (CH, 64), 0)
        parts = []
        for n in range(8):
            offset = n // 2 + 4 * (n % 2)
            part = jnp.where(chip + offset < chips, inverse[:, 64 * n : 64 * n + 64], 0.0)
            if offset == 0:
                after = jnp.where(chip + 8 < chips, inverse[:, BAND:], 0.0)
                part = jnp.where(column >= 32 * core + channel, part, after)
            parts.append(part)
        whole = jnp.concatenate(parts, 1)
        for c in range(CH):
            inverse_ref[c] = whole[c : c + 1]

    def one_channel(c):
        lags = jnp.dot(
            weights_ref[...],
            product_ref[pl.ds(pl.multiple_of(c * FBINS, FBINS), FBINS), :],
            preferred_element_type=jnp.float32,
        )
        lags = (lags * inverse_ref[c]).astype(jnp.bfloat16)
        tiles = [lags[:, 128 * j : 128 * j + 128] for j in range(LINE)]
        shift = 32 * core + c
        low = [pltpu.roll(tile, (128 - shift) % 128, 1) for tile in tiles]
        high = [pltpu.roll(tile, 64 - shift, 1) for tile in tiles]
        lane = lax.broadcasted_iota(jnp.int32, (LAGS, 128), 1)
        first, second = lane < 64 - shift, lane < 128 - shift
        rows = pl.ds(pl.multiple_of(c % BATCH * LAGS, LAGS), LAGS)
        for u, (one, two, three) in enumerate(
            (
                (low[0], high[1], low[2]),
                (low[2], high[3], high[0]),
                (high[0], low[1], high[2]),
                (high[2], low[3], low[0]),
            )
        ):
            result_ref[c // BATCH, u, rows, :] = jnp.where(first, one, jnp.where(second, two, three))

    def flush(batch, chunk):
        at = pl.multiple_of(chunk * CHUNK, CHUNK)
        for u in range(4):
            block = jnp.stack(
                [result_ref[batch, u, pl.ds(n * LAGS + at, CHUNK), :] for n in range(BATCH)]
            ).astype(jnp.float32)
            staging_ref[pl.ds(at, CHUNK), :, u * 128 : u * 128 + 128] = jnp.swapaxes(
                block, 0, 1
            ).astype(jnp.bfloat16)

    def leaving(batch, chunk):
        at = pl.multiple_of(chunk * CHUNK, CHUNK)
        return pltpu.make_async_copy(
            staging_ref.at[pl.ds(at, CHUNK)],
            out_ref.at[pl.ds(at, CHUNK), pl.ds(batch * BATCH, BATCH), :],
            out_sems.at[chunk],
        )

    lag_step = step - corr_steps
    batch_steps = BATCH // CSTEP

    @pl.when(jnp.logical_and(step >= corr_steps, lag_step < batch_steps))
    def first_batch():
        lax.fori_loop(0, CSTEP, lambda n, carry: one_channel(lag_step * CSTEP + n), None, unroll=CSTEP)

    @pl.when(lag_step >= batch_steps)
    def second_batch():
        def one(n, carry):
            c = lag_step * CSTEP + n
            one_channel(c)
            flush(0, c - BATCH)
            leaving(0, c - BATCH).start()

        lax.fori_loop(0, CSTEP, one, None, unroll=CSTEP)

    @pl.when(lag_step == 2 * batch_steps - 1)
    def last_flush():
        def one(n, carry):
            leaving(0, n).wait()
            flush(1, n)
            leaving(1, n).start()

        lax.fori_loop(0, LAGS // CHUNK, one, None, unroll=2)
        lax.fori_loop(0, LAGS // CHUNK, lambda n, carry: leaving(1, n).wait(), None)


def band_lags(place, own, sources, arrays, lies, table):
    corr_steps = GROUPS // STEP
    blocks = sum(map(len, lies))
    source_spec = pl.BlockSpec((STEP, CH, DEPTH), lambda i: (jnp.minimum(i, corr_steps - 1), 0, 0))
    flops = 2 * CH * FBINS * BAND * (DEPTH + LAGS)
    moved_bytes = 2 * blocks * CH * DEPTH * GROUPS + 2 * CH * LAGS * BAND
    return pl.pallas_call(
        lambda *refs: band_kernel(lies, *refs),
        grid=(corr_steps + CH // CSTEP,),
        out_shape=jax.ShapeDtypeStruct((LAGS, CH, BAND), jnp.bfloat16),
        in_specs=[
            pl.BlockSpec(memory_space=pltpu.SMEM),
            pl.BlockSpec((1, CH, DEPTH), lambda i: (GROUPS, 0, 0)),
            source_spec,
            source_spec,
        ]
        + [pl.BlockSpec(memory_space=pl.ANY)] * (len(arrays) + 1),
        out_specs=pl.BlockSpec(memory_space=pl.ANY),
        scratch_shapes=[
            pltpu.VMEM((2, blocks, STEP, CH, DEPTH), jnp.bfloat16),
            pltpu.VMEM((blocks, CH, DEPTH), jnp.bfloat16),
            pltpu.VMEM((2, CH * GROUP, DEPTH), jnp.bfloat16),
            pltpu.VMEM((CH * FBINS, BAND), jnp.bfloat16),
            pltpu.VMEM((CH, 1, BAND), jnp.float32),
            pltpu.VMEM((LAGS, FBINS), jnp.bfloat16),
            pltpu.VMEM((2, 4, BATCH * LAGS, 128), jnp.bfloat16),
            pltpu.VMEM((LAGS, BATCH, BAND), jnp.bfloat16),
            pltpu.SemaphoreType.DMA((4,)),
            pltpu.SemaphoreType.DMA((LAGS // CHUNK,)),
        ],
        compiler_params=pltpu.CompilerParams(
            vmem_limit_bytes=VMEM, dimension_semantics=("arbitrary",)
        ),
        cost_estimate=pl.CostEstimate(flops=flops, bytes_accessed=moved_bytes, transcendentals=0),
        name="band_lags",
    )(place, own, *sources, *arrays, table)


def lag_table():
    lag_index = np.arange(LAGS, dtype=np.int64)
    tables = []
    for rank in range(2):
        freq_index = (np.arange(FBINS, dtype=np.int64) + rank * BINS) % FBINS
        angles = (lag_index[:, None] * freq_index[None, :] % NFFT) * (2.0 * math.pi / NFFT)
        values = -np.sin(angles) if rank else np.cos(angles)
        tables.append((values * FBINS ** (-0.5)).astype(np.float32).astype(ml_dtypes.bfloat16))
    return np.stack(tables)


def local(spectra, seg_mask):
    chan = lax.axis_index("chan")
    rank = lax.axis_index("freq")
    core, x, row = chan % 2, chan // 2 % LINE, chan // (2 * LINE) % ROWS
    chips = lax.axis_size("chan") // 2
    place = jnp.stack([core, x, chan // 2, jnp.int32(chips), rank]).astype(jnp.int32)
    edge = jnp.where(rank == 0, spectra[..., BINS - 128 :], spectra[..., :128])
    rim = moved(edge, freq=1)
    own = whiten(rank.astype(jnp.int32).reshape(1), spectra, rim, seg_mask)

    def along(block, j):
        return moved(block, (0, 0, j))

    def flip(block):
        return moved(block, freq=1)

    def swap(block):
        return moved(block, core=1)

    def reached(j):
        return along(jnp.where(x >= j, own, after), j)

    after = moved(own, (1, 0, 0))
    own_flip = flip(own)
    own, after = lax.optimization_barrier((own, after))
    crossing = jnp.where(row == 1, own, after)
    one, three = reached(1), reached(3)
    cross = moved(crossing, (0, 1, 0))
    cross_flip = moved(crossing, (0, 1, 0), freq=1)
    one, three, cross, cross_flip, own_flip = lax.optimization_barrier(
        (one, three, cross, cross_flip, own_flip)
    )
    pairs = {0: jnp.stack([cross, cross_flip])}
    row_pair = jnp.stack([one, three])
    row_flip = flip(row_pair)
    pairs[1], pairs[3] = along(pairs[0], 1), along(pairs[0], 3)
    two = reached(2)
    after_flip = moved(own_flip, (1, 0, 0))
    singles = [own, own_flip, after, after_flip]
    row_flip, row_pair_, pair_, *singles_ = lax.optimization_barrier(
        (row_flip, row_pair, pairs[0], *singles)
    )
    swapped = [swap(block) for block in (*singles_, pair_, row_pair_, row_flip)]
    pairs[1], pairs[3], two = lax.optimization_barrier((pairs[1], pairs[3], two))
    two_flip = flip(two)
    cross_two = along(pairs[1][0], 1)
    cross_two_flip = along(pairs[3][1], 3)
    held = [*singles, pairs[0], row_pair, row_flip, pairs[1], pairs[3]]
    held += [two, two_flip, cross_two, cross_two_flip]
    swapped = [*swapped, *(swap(block) for block in held[7:])]
    names = [[(0, 0, 0)], [(0, 0, 1)], [(0, 2, 0)], [(0, 2, 1)], [(0, 1, 0), (0, 1, 1)]]
    names += [[(1, 0, 0), (3, 0, 0)], [(1, 0, 1), (3, 0, 1)]]
    names += [[(1, 1, 0), (1, 1, 1)], [(3, 1, 0), (3, 1, 1)]]
    names += [[(2, 0, 0)], [(2, 0, 1)], [(2, 1, 0)], [(2, 1, 1)]]
    arrays, lies = [], []
    for layer, blocks in enumerate((held, swapped)):
        for listed, block in zip(names, blocks):
            arrays.append(block if block.ndim == 4 else block[None])
            lies.append([(*name, layer) for name in listed])
    table = jnp.asarray(lag_table())
    return band_lags(place, own, [own, own_flip], arrays, lies, table)[None]


def solution(mesh):
    placed = (P(None, None, "chan", "freq"), P("chan", None))
    return jax.shard_map(
        local, mesh=mesh, in_specs=placed, out_specs=P("freq", None, "chan", None), check_vma=False
    )
```

```python
import math

import jax
import jax.numpy as jnp
import ml_dtypes
import numpy as np
from jax import lax
from jax.experimental import pallas as pl
from jax.experimental.pallas import tpu as pltpu
from jax.sharding import PartitionSpec as P

BAND = 512
FBINS = 1024
HALF = 64
LAGS = 256
NFFT = 2048
EPSILON = 1e-06
SEGMENTS = 8
CH = 32
BINS = 512
GROUP = 16
GROUPS = BINS // GROUP
DEPTH = 2 * SEGMENTS * GROUP
STEP = 8
UNROLL = 8
BATCH = 16
CHUNK = 16
ROWS = 2
LINE = 4
CSTEP = 8
AXES = ("chan", "freq")
VMEM = 60 * 1024 * 1024
INTERPRET = False


def moved(value, back=(0, 0, 0), core=0, freq=0):
    count, halves = lax.axis_size("chan"), lax.axis_size("freq")
    planes = count // (ROWS * LINE * 2)
    pairs = []
    for index in range(count * halves):
        rest, f = divmod(index, halves)
        rest, k = divmod(rest, 2)
        rest, x = divmod(rest, LINE)
        z, y = divmod(rest, ROWS)
        z, y, x = (z - back[0]) % planes, (y - back[1]) % ROWS, (x - back[2]) % LINE
        pairs.append((index, (((z * ROWS + y) * LINE + x) * 2 + (k ^ core)) * halves + (f ^ freq)))
    return lax.ppermute(value, AXES, pairs)


def whiten_kernel(rank_ref, spectra_ref, rim_ref, mask_ref, out_ref):
    rank = rank_ref[0]
    real = spectra_ref[0].astype(jnp.float32)
    imag = spectra_ref[1].astype(jnp.float32)
    magnitude = jnp.sqrt(real * real + imag * imag).reshape(SEGMENTS * CH, BINS)
    rim_real = rim_ref[0].astype(jnp.float32)
    rim_imag = rim_ref[1].astype(jnp.float32)
    rim = jnp.sqrt(rim_real * rim_real + rim_imag * rim_imag).reshape(SEGMENTS * CH, 128)

    def window_sum(values, positions):
        target = lax.broadcasted_iota(jnp.int32, (values.shape[1], BINS), 1)
        near = jnp.abs(positions - target) <= HALF
        table = jnp.where(near, 1.0, 0.0).astype(jnp.bfloat16)
        high = values.astype(jnp.bfloat16)
        low = (values - high.astype(jnp.float32)).astype(jnp.bfloat16)
        return jnp.dot(high, table, preferred_element_type=jnp.float32) + jnp.dot(
            low, table, preferred_element_type=jnp.float32
        )

    inner = lax.broadcasted_iota(jnp.int32, (BINS, BINS), 0)
    outer = lax.broadcasted_iota(jnp.int32, (128, BINS), 0) + jnp.where(rank == 0, BINS, -128)
    summed = window_sum(magnitude, inner) + window_sum(rim, outer)
    bin_index = rank * BINS + lax.broadcasted_iota(jnp.int32, (1, BINS), 1)
    counted = (
        jnp.minimum(bin_index + HALF, FBINS - 1) - jnp.maximum(bin_index - HALF, 0) + 1
    ).astype(jnp.float32)
    levels = summed / counted + EPSILON
    scale = (1.0 / levels).reshape(SEGMENTS, CH, BINS)
    valid = mask_ref[...].astype(jnp.float32)
    out_ref[GROUPS] = jnp.concatenate(
        [valid, jnp.zeros((CH, DEPTH - SEGMENTS), jnp.float32)], 1
    ).astype(jnp.bfloat16)
    lane = lax.broadcasted_iota(jnp.int32, (CH, 128), 1)
    for p, part in enumerate((real, imag)):
        for tile in range(BINS // 128):
            cut = slice(tile * 128, tile * 128 + 128)
            rows = [
                part[s, :, cut] * scale[s, :, cut] * valid[:, s : s + 1] for s in range(SEGMENTS)
            ]
            for bit in (1, 2, 4):
                upper = (lane // GROUP) & bit != 0
                for i in range(SEGMENTS):
                    if i & bit:
                        continue
                    a, b = rows[i], rows[i + bit]
                    rows[i] = jnp.where(upper, pltpu.roll(b, bit * GROUP, 1), a)
                    rows[i + bit] = jnp.where(upper, b, pltpu.roll(a, 128 - bit * GROUP, 1))
            for g in range(SEGMENTS):
                out_ref[tile * SEGMENTS + g, :, p * 128 : p * 128 + 128] = rows[g].astype(
                    jnp.bfloat16
                )


def whiten(rank, spectra, rim, mask):
    return pl.pallas_call(
        whiten_kernel,
        out_shape=jax.ShapeDtypeStruct((GROUPS + 1, CH, DEPTH), jnp.bfloat16),
        in_specs=[pl.BlockSpec(memory_space=pltpu.SMEM)]
        + [pl.BlockSpec(memory_space=pltpu.VMEM)] * 3,
        out_specs=pl.BlockSpec(memory_space=pltpu.VMEM),
        compiler_params=pltpu.CompilerParams(vmem_limit_bytes=VMEM),
        name="whiten",
    )(rank, spectra, rim, mask)


def band_kernel(lies, place_ref, *refs):
    own_ref, source_refs, array_refs = refs[0], refs[1:3], refs[3 : 3 + len(lies)]
    (table_ref, out_ref, rows_ref, flags_ref, diagonal_ref, product_ref, inverse_ref) = refs[
        3 + len(lies) : 10 + len(lies)
    ]
    weights_ref, result_ref, staging_ref, sems, out_sems = refs[10 + len(lies) :]
    core, x, chip, chips, rank = [place_ref[n] for n in range(5)]
    step = pl.program_id(0)
    corr_steps = GROUPS // STEP
    place = {}
    count = 0
    spans = []
    for names in lies:
        spans.append((count, len(names)))
        for name in names:
            place[name] = count
            count += 1

    def order(half):
        listed = []

        def add(kinds, layer):
            listed.append(jnp.where(layer == 0, place[(*kinds, 0)], place[(*kinds, 1)]))

        for j in range(LINE):
            wraps = x + j >= LINE
            for upper in (0, 1):
                for layer in (core, 1 - core):
                    straight = [place[j, upper, half, n] for n in range(2)]
                    turned = [place[j, 1 - upper, half, n] for n in range(2)]
                    listed.append(
                        jnp.where(
                            wraps,
                            jnp.where(layer == 0, turned[0], turned[1]),
                            jnp.where(layer == 0, straight[0], straight[1]),
                        )
                    )
        for layer in (core, 1 - core):
            add((0, 2, half), layer)
        return listed

    def fetch(number):
        slot = number % 2
        for ref, (start, size) in zip(array_refs, spans):
            pltpu.make_async_copy(
                ref.at[:, pl.ds(number * STEP, STEP)],
                rows_ref.at[slot, pl.ds(start, size)],
                sems.at[slot],
            ).start()

    @pl.when(step == 0)
    def begin():
        fetch(0)
        pltpu.make_async_copy(table_ref.at[rank], weights_ref, sems.at[3]).start()
        for ref, (start, size) in zip(array_refs, spans):
            pltpu.make_async_copy(
                ref.at[:, GROUPS], flags_ref.at[pl.ds(start, size)], sems.at[2]
            ).start()

    @pl.when(step < corr_steps)
    def correlate():
        @pl.when(step + 1 < corr_steps)
        def ahead():
            fetch(step + 1)

        slot = step % 2
        pltpu.make_async_copy(rows_ref.at[slot], rows_ref.at[slot], sems.at[slot]).wait()
        lane_bin = lax.broadcasted_iota(jnp.int32, (GROUP, DEPTH), 1) % GROUP
        own_bin = lane_bin == lax.broadcasted_iota(jnp.int32, (GROUP, DEPTH), 0)
        column = lax.broadcasted_iota(jnp.int32, (GROUP, 128), 1)
        orders = [order(half) for half in range(2)]

        def one_group(index, carry):
            for half in range(2):
                source = source_refs[half][index].astype(jnp.float32)
                real, imag = source[:, : DEPTH // 2], source[:, DEPTH // 2 :]
                source = jnp.concatenate(
                    [jnp.where(rank == 0, real, -imag), jnp.where(rank == 0, imag, real)], 1
                )
                for c in range(CH):
                    spread = jnp.broadcast_to(source[c : c + 1, :], (GROUP, DEPTH))
                    diagonal_ref[half, c * GROUP : (c + 1) * GROUP, :] = jnp.where(
                        own_bin, spread, 0.0
                    ).astype(jnp.bfloat16)
                rows = jnp.concatenate([rows_ref[slot, at, index] for at in orders[half]], 0)
                product = lax.dot_general(
                    diagonal_ref[half],
                    rows,
                    (((1,), (1,)), ((), ())),
                    preferred_element_type=jnp.float32,
                )
                first_bin = pl.multiple_of(half * BINS + (step * STEP + index) * GROUP, GROUP)
                for c in range(CH):
                    part = product[c * GROUP : (c + 1) * GROUP]
                    here = pl.ds(c * FBINS + first_bin, GROUP)
                    tail = jnp.concatenate([part[:, BAND:], part[:, 64:128]], 1)
                    head = jnp.where(column >= 32 * core + c, part[:, :128], tail)
                    product_ref[here, :] = jnp.concatenate([head, part[:, 128:BAND]], 1).astype(
                        jnp.bfloat16
                    )
            return carry

        lax.fori_loop(0, STEP, one_group, 0, unroll=UNROLL)

    @pl.when(step == corr_steps)
    def scales():
        pltpu.make_async_copy(table_ref.at[rank], weights_ref, sems.at[3]).wait()
        pltpu.make_async_copy(flags_ref, flags_ref, sems.at[2]).wait()
        counts = lax.dot_general(
            own_ref[0],
            jnp.concatenate([flags_ref[at] for at in order(0)], 0),
            (((1,), (1,)), ((), ())),
            preferred_element_type=jnp.float32,
        )
        inverse = 1.0 / jnp.maximum(counts, 1.0)
        column = lax.broadcasted_iota(jnp.int32, (CH, 64), 1)
        channel = lax.broadcasted_iota(jnp.int32, (CH, 64), 0)
        parts = []
        for n in range(8):
            offset = n // 2 + 4 * (n % 2)
            part = jnp.where(chip + offset < chips, inverse[:, 64 * n : 64 * n + 64], 0.0)
            if offset == 0:
                after = jnp.where(chip + 8 < chips, inverse[:, BAND:], 0.0)
                part = jnp.where(column >= 32 * core + channel, part, after)
            parts.append(part)
        whole = jnp.concatenate(parts, 1)
        for c in range(CH):
            inverse_ref[c] = whole[c : c + 1]

    def one_channel(c):
        lags = jnp.dot(
            weights_ref[...],
            product_ref[pl.ds(pl.multiple_of(c * FBINS, FBINS), FBINS), :],
            preferred_element_type=jnp.float32,
        )
        lags = (lags * inverse_ref[c]).astype(jnp.bfloat16)
        tiles = [lags[:, 128 * j : 128 * j + 128] for j in range(LINE)]
        shift = 32 * core + c
        low = [pltpu.roll(tile, (128 - shift) % 128, 1) for tile in tiles]
        high = [pltpu.roll(tile, 64 - shift, 1) for tile in tiles]
        lane = lax.broadcasted_iota(jnp.int32, (LAGS, 128), 1)
        first, second = lane < 64 - shift, lane < 128 - shift
        rows = pl.ds(pl.multiple_of(c % BATCH * LAGS, LAGS), LAGS)
        for u, (one, two, three) in enumerate(
            (
                (low[0], high[1], low[2]),
                (low[2], high[3], high[0]),
                (high[0], low[1], high[2]),
                (high[2], low[3], low[0]),
            )
        ):
            result_ref[c // BATCH, u, rows, :] = jnp.where(first, one, jnp.where(second, two, three))

    def flush(batch, chunk):
        at = pl.multiple_of(chunk * CHUNK, CHUNK)
        for u in range(4):
            block = jnp.stack(
                [result_ref[batch, u, pl.ds(n * LAGS + at, CHUNK), :] for n in range(BATCH)]
            ).astype(jnp.float32)
            staging_ref[pl.ds(at, CHUNK), :, u * 128 : u * 128 + 128] = jnp.swapaxes(
                block, 0, 1
            ).astype(jnp.bfloat16)

    def leaving(batch, chunk):
        at = pl.multiple_of(chunk * CHUNK, CHUNK)
        return pltpu.make_async_copy(
            staging_ref.at[pl.ds(at, CHUNK)],
            out_ref.at[pl.ds(at, CHUNK), pl.ds(batch * BATCH, BATCH), :],
            out_sems.at[chunk],
        )

    lag_step = step - corr_steps
    batch_steps = BATCH // CSTEP

    @pl.when(jnp.logical_and(step >= corr_steps, lag_step < batch_steps))
    def first_batch():
        lax.fori_loop(0, CSTEP, lambda n, carry: one_channel(lag_step * CSTEP + n), None, unroll=CSTEP)

    @pl.when(lag_step >= batch_steps)
    def second_batch():
        def one(n, carry):
            c = lag_step * CSTEP + n
            one_channel(c)
            flush(0, c - BATCH)
            leaving(0, c - BATCH).start()

        lax.fori_loop(0, CSTEP, one, None, unroll=CSTEP)

    @pl.when(lag_step == 2 * batch_steps - 1)
    def last_flush():
        def one(n, carry):
            leaving(0, n).wait()
            flush(1, n)
            leaving(1, n).start()

        lax.fori_loop(0, LAGS // CHUNK, one, None, unroll=2)
        lax.fori_loop(0, LAGS // CHUNK, lambda n, carry: leaving(1, n).wait(), None)


def band_lags(place, own, sources, arrays, lies, table):
    corr_steps = GROUPS // STEP
    blocks = sum(map(len, lies))
    source_spec = pl.BlockSpec((STEP, CH, DEPTH), lambda i: (jnp.minimum(i, corr_steps - 1), 0, 0))
    flops = 2 * CH * FBINS * BAND * (DEPTH + LAGS)
    moved_bytes = 2 * blocks * CH * DEPTH * GROUPS + 2 * CH * LAGS * BAND
    return pl.pallas_call(
        lambda *refs: band_kernel(lies, *refs),
        grid=(corr_steps + CH // CSTEP,),
        out_shape=jax.ShapeDtypeStruct((LAGS, CH, BAND), jnp.bfloat16),
        in_specs=[
            pl.BlockSpec(memory_space=pltpu.SMEM),
            pl.BlockSpec((1, CH, DEPTH), lambda i: (GROUPS, 0, 0)),
            source_spec,
            source_spec,
        ]
        + [pl.BlockSpec(memory_space=pl.ANY)] * (len(arrays) + 1),
        out_specs=pl.BlockSpec(memory_space=pl.ANY),
        scratch_shapes=[
            pltpu.VMEM((2, blocks, STEP, CH, DEPTH), jnp.bfloat16),
            pltpu.VMEM((blocks, CH, DEPTH), jnp.bfloat16),
            pltpu.VMEM((2, CH * GROUP, DEPTH), jnp.bfloat16),
            pltpu.VMEM((CH * FBINS, BAND), jnp.bfloat16),
            pltpu.VMEM((CH, 1, BAND), jnp.float32),
            pltpu.VMEM((LAGS, FBINS), jnp.bfloat16),
            pltpu.VMEM((2, 4, BATCH * LAGS, 128), jnp.bfloat16),
            pltpu.VMEM((LAGS, BATCH, BAND), jnp.bfloat16),
            pltpu.SemaphoreType.DMA((4,)),
            pltpu.SemaphoreType.DMA((LAGS // CHUNK,)),
        ],
        compiler_params=pltpu.CompilerParams(
            vmem_limit_bytes=VMEM, dimension_semantics=("arbitrary",)
        ),
        cost_estimate=pl.CostEstimate(flops=flops, bytes_accessed=moved_bytes, transcendentals=0),
        name="band_lags",
    )(place, own, *sources, *arrays, table)


def lag_table():
    lag_index = np.arange(LAGS, dtype=np.int64)
    tables = []
    for rank in range(2):
        freq_index = (np.arange(FBINS, dtype=np.int64) + rank * BINS) % FBINS
        angles = (lag_index[:, None] * freq_index[None, :] % NFFT) * (2.0 * math.pi / NFFT)
        values = -np.sin(angles) if rank else np.cos(angles)
        tables.append((values * FBINS ** (-0.5)).astype(np.float32).astype(ml_dtypes.bfloat16))
    return np.stack(tables)


def local(spectra, seg_mask):
    chan = lax.axis_index("chan")
    rank = lax.axis_index("freq")
    core, x, row = chan % 2, chan // 2 % LINE, chan // (2 * LINE) % ROWS
    chips = lax.axis_size("chan") // 2
    place = jnp.stack([core, x, chan // 2, jnp.int32(chips), rank]).astype(jnp.int32)
    edge = jnp.where(rank == 0, spectra[..., BINS - 128 :], spectra[..., :128])
    rim = moved(edge, freq=1)
    own = whiten(rank.astype(jnp.int32).reshape(1), spectra, rim, seg_mask)

    def along(block, j):
        return moved(block, (0, 0, j))

    def flip(block):
        return moved(block, freq=1)

    def swap(block):
        return moved(block, core=1)

    def reached(j):
        return along(jnp.where(x >= j, own, after), j)

    after = moved(own, (1, 0, 0))
    own_flip = flip(own)
    own, after = lax.optimization_barrier((own, after))
    crossing = jnp.where(row == 1, own, after)
    one, three = reached(1), reached(3)
    cross = moved(crossing, (0, 1, 0))
    cross_flip = moved(crossing, (0, 1, 0), freq=1)
    one, three, cross, cross_flip, own_flip = lax.optimization_barrier(
        (one, three, cross, cross_flip, own_flip)
    )
    pairs = {0: jnp.stack([cross, cross_flip])}
    row_pair = jnp.stack([one, three])
    row_flip = flip(row_pair)
    pairs[1], pairs[3] = along(pairs[0], 1), along(pairs[0], 3)
    two = reached(2)
    after_flip = moved(own_flip, (1, 0, 0))
    row_flip, after_flip, *gated = lax.optimization_barrier(
        (row_flip, after_flip, own, own_flip, after, pairs[0], row_pair)
    )
    swapped = [
        swap(jnp.stack([*gated[:3], after_flip])),
        swap(jnp.concatenate([*gated[3:], row_flip])),
    ]
    pairs[1], pairs[3], two = lax.optimization_barrier((pairs[1], pairs[3], two))
    two_flip = flip(two)
    cross_two = along(pairs[1][0], 1)
    cross_two_flip = along(pairs[3][1], 3)
    late = lax.optimization_barrier(
        (pairs[1], pairs[3], two, two_flip, cross_two, cross_two_flip)
    )
    swapped += [swap(block) for block in late]
    held = [own, own_flip, after, after_flip, pairs[0], row_pair, row_flip, *late]
    one_by_one = [[(0, 0, 0)], [(0, 0, 1)], [(0, 2, 0)], [(0, 2, 1)]]
    in_pairs = [[(0, 1, 0), (0, 1, 1)], [(1, 0, 0), (3, 0, 0)], [(1, 0, 1), (3, 0, 1)]]
    rest = [[(1, 1, 0), (1, 1, 1)], [(3, 1, 0), (3, 1, 1)]]
    rest += [[(2, 0, 0)], [(2, 0, 1)], [(2, 1, 0)], [(2, 1, 1)]]
    arrays, lies = [], []
    for layer, blocks, names in (
        (0, held, one_by_one + in_pairs + rest),
        (1, swapped, [sum(one_by_one, []), sum(in_pairs, [])] + rest),
    ):
        for listed, block in zip(names, blocks):
            arrays.append(block if block.ndim == 4 else block[None])
            lies.append([(*name, layer) for name in listed])
    table = jnp.asarray(lag_table())
    return band_lags(place, own, [own, own_flip], arrays, lies, table)[None]


def solution(mesh):
    placed = (P(None, None, "chan", "freq"), P("chan", None))
    return jax.shard_map(
        local, mesh=mesh, in_specs=placed, out_specs=P("freq", None, "chan", None), check_vma=False
    )
```

```python
import math

import jax
import jax.numpy as jnp
import ml_dtypes
import numpy as np
from jax import lax
from jax.experimental import pallas as pl
from jax.experimental.pallas import tpu as pltpu
from jax.sharding import PartitionSpec as P

BAND = 512
FBINS = 1024
HALF = 64
LAGS = 256
NFFT = 2048
EPSILON = 1e-06
SEGMENTS = 8
CH = 32
BINS = 512
GROUP = 16
GROUPS = BINS // GROUP
DEPTH = 2 * SEGMENTS * GROUP
STEP = 8
UNROLL = 8
BATCH = 16
CHUNK = 16
ROWS = 2
LINE = 4
CSTEP = 8
AXES = ("chan", "freq")
VMEM = 60 * 1024 * 1024
INTERPRET = False


def moved(value, back=(0, 0, 0), core=0, freq=0):
    count, halves = lax.axis_size("chan"), lax.axis_size("freq")
    planes = count // (ROWS * LINE * 2)
    pairs = []
    for index in range(count * halves):
        rest, f = divmod(index, halves)
        rest, k = divmod(rest, 2)
        rest, x = divmod(rest, LINE)
        z, y = divmod(rest, ROWS)
        z, y, x = (z - back[0]) % planes, (y - back[1]) % ROWS, (x - back[2]) % LINE
        pairs.append((index, (((z * ROWS + y) * LINE + x) * 2 + (k ^ core)) * halves + (f ^ freq)))
    return lax.ppermute(value, AXES, pairs)


def whiten_kernel(rank_ref, spectra_ref, rim_ref, mask_ref, out_ref):
    rank = rank_ref[0]
    real = spectra_ref[0].astype(jnp.float32)
    imag = spectra_ref[1].astype(jnp.float32)
    magnitude = jnp.sqrt(real * real + imag * imag).reshape(SEGMENTS * CH, BINS)
    rim_real = rim_ref[0].astype(jnp.float32)
    rim_imag = rim_ref[1].astype(jnp.float32)
    rim = jnp.sqrt(rim_real * rim_real + rim_imag * rim_imag).reshape(SEGMENTS * CH, 128)

    def window_sum(values, positions):
        target = lax.broadcasted_iota(jnp.int32, (values.shape[1], BINS), 1)
        near = jnp.abs(positions - target) <= HALF
        table = jnp.where(near, 1.0, 0.0).astype(jnp.bfloat16)
        high = values.astype(jnp.bfloat16)
        low = (values - high.astype(jnp.float32)).astype(jnp.bfloat16)
        return jnp.dot(high, table, preferred_element_type=jnp.float32) + jnp.dot(
            low, table, preferred_element_type=jnp.float32
        )

    inner = lax.broadcasted_iota(jnp.int32, (BINS, BINS), 0)
    outer = lax.broadcasted_iota(jnp.int32, (128, BINS), 0) + jnp.where(rank == 0, BINS, -128)
    summed = window_sum(magnitude, inner) + window_sum(rim, outer)
    bin_index = rank * BINS + lax.broadcasted_iota(jnp.int32, (1, BINS), 1)
    counted = (
        jnp.minimum(bin_index + HALF, FBINS - 1) - jnp.maximum(bin_index - HALF, 0) + 1
    ).astype(jnp.float32)
    levels = summed / counted + EPSILON
    scale = (1.0 / levels).reshape(SEGMENTS, CH, BINS)
    valid = mask_ref[...].astype(jnp.float32)
    out_ref[GROUPS] = jnp.concatenate(
        [valid, jnp.zeros((CH, DEPTH - SEGMENTS), jnp.float32)], 1
    ).astype(jnp.bfloat16)
    lane = lax.broadcasted_iota(jnp.int32, (CH, 128), 1)
    for p, part in enumerate((real, imag)):
        for tile in range(BINS // 128):
            cut = slice(tile * 128, tile * 128 + 128)
            rows = [
                part[s, :, cut] * scale[s, :, cut] * valid[:, s : s + 1] for s in range(SEGMENTS)
            ]
            for bit in (1, 2, 4):
                upper = (lane // GROUP) & bit != 0
                for i in range(SEGMENTS):
                    if i & bit:
                        continue
                    a, b = rows[i], rows[i + bit]
                    rows[i] = jnp.where(upper, pltpu.roll(b, bit * GROUP, 1), a)
                    rows[i + bit] = jnp.where(upper, b, pltpu.roll(a, 128 - bit * GROUP, 1))
            for g in range(SEGMENTS):
                out_ref[tile * SEGMENTS + g, :, p * 128 : p * 128 + 128] = rows[g].astype(
                    jnp.bfloat16
                )


def whiten(rank, spectra, rim, mask):
    return pl.pallas_call(
        whiten_kernel,
        out_shape=jax.ShapeDtypeStruct((GROUPS + 1, CH, DEPTH), jnp.bfloat16),
        in_specs=[pl.BlockSpec(memory_space=pltpu.SMEM)]
        + [pl.BlockSpec(memory_space=pltpu.VMEM)] * 3,
        out_specs=pl.BlockSpec(memory_space=pltpu.VMEM),
        compiler_params=pltpu.CompilerParams(vmem_limit_bytes=VMEM),
        name="whiten",
    )(rank, spectra, rim, mask)


def band_kernel(lies, place_ref, *refs):
    own_ref, source_refs, array_refs = refs[0], refs[1:3], refs[3 : 3 + len(lies)]
    (table_ref, out_ref, rows_ref, flags_ref, diagonal_ref, product_ref, inverse_ref) = refs[
        3 + len(lies) : 10 + len(lies)
    ]
    weights_ref, result_ref, staging_ref, sems, out_sems = refs[10 + len(lies) :]
    core, x, chip, chips, rank = [place_ref[n] for n in range(5)]
    step = pl.program_id(0)
    corr_steps = GROUPS // STEP
    place = {}
    count = 0
    spans = []
    for names in lies:
        spans.append((count, len(names)))
        for name in names:
            place[name] = count
            count += 1

    def order(half):
        listed = []

        def add(kinds, layer):
            listed.append(jnp.where(layer == 0, place[(*kinds, 0)], place[(*kinds, 1)]))

        for j in range(LINE):
            wraps = x + j >= LINE
            for upper in (0, 1):
                for layer in (core, 1 - core):
                    straight = [place[j, upper, half, n] for n in range(2)]
                    turned = [place[j, 1 - upper, half, n] for n in range(2)]
                    listed.append(
                        jnp.where(
                            wraps,
                            jnp.where(layer == 0, turned[0], turned[1]),
                            jnp.where(layer == 0, straight[0], straight[1]),
                        )
                    )
        for layer in (core, 1 - core):
            add((0, 2, half), layer)
        return listed

    def fetch(number):
        slot = number % 2
        for ref, (start, size) in zip(array_refs, spans):
            pltpu.make_async_copy(
                ref.at[:, pl.ds(number * STEP, STEP)],
                rows_ref.at[slot, pl.ds(start, size)],
                sems.at[slot],
            ).start()

    @pl.when(step == 0)
    def begin():
        fetch(0)
        pltpu.make_async_copy(table_ref.at[rank], weights_ref, sems.at[3]).start()
        for ref, (start, size) in zip(array_refs, spans):
            pltpu.make_async_copy(
                ref.at[:, GROUPS], flags_ref.at[pl.ds(start, size)], sems.at[2]
            ).start()

    @pl.when(step < corr_steps)
    def correlate():
        @pl.when(step + 1 < corr_steps)
        def ahead():
            fetch(step + 1)

        slot = step % 2
        pltpu.make_async_copy(rows_ref.at[slot], rows_ref.at[slot], sems.at[slot]).wait()
        lane_bin = lax.broadcasted_iota(jnp.int32, (GROUP, DEPTH), 1) % GROUP
        own_bin = lane_bin == lax.broadcasted_iota(jnp.int32, (GROUP, DEPTH), 0)
        column = lax.broadcasted_iota(jnp.int32, (GROUP, 128), 1)
        orders = [order(half) for half in range(2)]

        def one_group(index, carry):
            for half in range(2):
                source = source_refs[half][index].astype(jnp.float32)
                real, imag = source[:, : DEPTH // 2], source[:, DEPTH // 2 :]
                source = jnp.concatenate(
                    [jnp.where(rank == 0, real, -imag), jnp.where(rank == 0, imag, real)], 1
                )
                for c in range(CH):
                    spread = jnp.broadcast_to(source[c : c + 1, :], (GROUP, DEPTH))
                    diagonal_ref[half, c * GROUP : (c + 1) * GROUP, :] = jnp.where(
                        own_bin, spread, 0.0
                    ).astype(jnp.bfloat16)
                rows = jnp.concatenate([rows_ref[slot, at, index] for at in orders[half]], 0)
                product = lax.dot_general(
                    diagonal_ref[half],
                    rows,
                    (((1,), (1,)), ((), ())),
                    preferred_element_type=jnp.float32,
                )
                first_bin = pl.multiple_of(half * BINS + (step * STEP + index) * GROUP, GROUP)
                for c in range(CH):
                    part = product[c * GROUP : (c + 1) * GROUP]
                    here = pl.ds(c * FBINS + first_bin, GROUP)
                    tail = jnp.concatenate([part[:, BAND:], part[:, 64:128]], 1)
                    head = jnp.where(column >= 32 * core + c, part[:, :128], tail)
                    product_ref[here, :] = jnp.concatenate([head, part[:, 128:BAND]], 1).astype(
                        jnp.bfloat16
                    )
            return carry

        lax.fori_loop(0, STEP, one_group, 0, unroll=UNROLL)

    @pl.when(step == corr_steps)
    def scales():
        pltpu.make_async_copy(table_ref.at[rank], weights_ref, sems.at[3]).wait()
        pltpu.make_async_copy(flags_ref, flags_ref, sems.at[2]).wait()
        counts = lax.dot_general(
            own_ref[0],
            jnp.concatenate([flags_ref[at] for at in order(0)], 0),
            (((1,), (1,)), ((), ())),
            preferred_element_type=jnp.float32,
        )
        inverse = 1.0 / jnp.maximum(counts, 1.0)
        column = lax.broadcasted_iota(jnp.int32, (CH, 64), 1)
        channel = lax.broadcasted_iota(jnp.int32, (CH, 64), 0)
        parts = []
        for n in range(8):
            offset = n // 2 + 4 * (n % 2)
            part = jnp.where(chip + offset < chips, inverse[:, 64 * n : 64 * n + 64], 0.0)
            if offset == 0:
                after = jnp.where(chip + 8 < chips, inverse[:, BAND:], 0.0)
                part = jnp.where(column >= 32 * core + channel, part, after)
            parts.append(part)
        whole = jnp.concatenate(parts, 1)
        for c in range(CH):
            inverse_ref[c] = whole[c : c + 1]

    def one_channel(c):
        lags = jnp.dot(
            weights_ref[...],
            product_ref[pl.ds(pl.multiple_of(c * FBINS, FBINS), FBINS), :],
            preferred_element_type=jnp.float32,
        )
        lags = (lags * inverse_ref[c]).astype(jnp.bfloat16)
        tiles = [lags[:, 128 * j : 128 * j + 128] for j in range(LINE)]
        shift = 32 * core + c
        low = [pltpu.roll(tile, (128 - shift) % 128, 1) for tile in tiles]
        high = [pltpu.roll(tile, 64 - shift, 1) for tile in tiles]
        lane = lax.broadcasted_iota(jnp.int32, (LAGS, 128), 1)
        first, second = lane < 64 - shift, lane < 128 - shift
        rows = pl.ds(pl.multiple_of(c % BATCH * LAGS, LAGS), LAGS)
        for u, (one, two, three) in enumerate(
            (
                (low[0], high[1], low[2]),
                (low[2], high[3], high[0]),
                (high[0], low[1], high[2]),
                (high[2], low[3], low[0]),
            )
        ):
            result_ref[c // BATCH, u, rows, :] = jnp.where(first, one, jnp.where(second, two, three))

    def flush(batch, chunk):
        at = pl.multiple_of(chunk * CHUNK, CHUNK)
        for u in range(4):
            block = jnp.stack(
                [result_ref[batch, u, pl.ds(n * LAGS + at, CHUNK), :] for n in range(BATCH)]
            ).astype(jnp.float32)
            staging_ref[pl.ds(at, CHUNK), :, u * 128 : u * 128 + 128] = jnp.swapaxes(
                block, 0, 1
            ).astype(jnp.bfloat16)

    def leaving(batch, chunk):
        at = pl.multiple_of(chunk * CHUNK, CHUNK)
        return pltpu.make_async_copy(
            staging_ref.at[pl.ds(at, CHUNK)],
            out_ref.at[pl.ds(at, CHUNK), pl.ds(batch * BATCH, BATCH), :],
            out_sems.at[chunk],
        )

    lag_step = step - corr_steps
    batch_steps = BATCH // CSTEP

    @pl.when(jnp.logical_and(step >= corr_steps, lag_step < batch_steps))
    def first_batch():
        lax.fori_loop(0, CSTEP, lambda n, carry: one_channel(lag_step * CSTEP + n), None, unroll=CSTEP)

    @pl.when(lag_step >= batch_steps)
    def second_batch():
        def one(n, carry):
            c = lag_step * CSTEP + n
            one_channel(c)
            flush(0, c - BATCH)
            leaving(0, c - BATCH).start()

        lax.fori_loop(0, CSTEP, one, None, unroll=CSTEP)

    @pl.when(lag_step == 2 * batch_steps - 1)
    def last_flush():
        def one(n, carry):
            leaving(0, n).wait()
            flush(1, n)
            leaving(1, n).start()

        lax.fori_loop(0, LAGS // CHUNK, one, None, unroll=2)
        lax.fori_loop(0, LAGS // CHUNK, lambda n, carry: leaving(1, n).wait(), None)


def band_lags(place, own, sources, arrays, lies, table):
    corr_steps = GROUPS // STEP
    blocks = sum(map(len, lies))
    source_spec = pl.BlockSpec((STEP, CH, DEPTH), lambda i: (jnp.minimum(i, corr_steps - 1), 0, 0))
    flops = 2 * CH * FBINS * BAND * (DEPTH + LAGS)
    moved_bytes = 2 * blocks * CH * DEPTH * GROUPS + 2 * CH * LAGS * BAND
    return pl.pallas_call(
        lambda *refs: band_kernel(lies, *refs),
        grid=(corr_steps + CH // CSTEP,),
        out_shape=jax.ShapeDtypeStruct((LAGS, CH, BAND), jnp.bfloat16),
        in_specs=[
            pl.BlockSpec(memory_space=pltpu.SMEM),
            pl.BlockSpec((1, CH, DEPTH), lambda i: (GROUPS, 0, 0)),
            source_spec,
            source_spec,
        ]
        + [pl.BlockSpec(memory_space=pl.ANY)] * (len(arrays) + 1),
        out_specs=pl.BlockSpec(memory_space=pl.ANY),
        scratch_shapes=[
            pltpu.VMEM((2, blocks, STEP, CH, DEPTH), jnp.bfloat16),
            pltpu.VMEM((blocks, CH, DEPTH), jnp.bfloat16),
            pltpu.VMEM((2, CH * GROUP, DEPTH), jnp.bfloat16),
            pltpu.VMEM((CH * FBINS, BAND), jnp.bfloat16),
            pltpu.VMEM((CH, 1, BAND), jnp.float32),
            pltpu.VMEM((LAGS, FBINS), jnp.bfloat16),
            pltpu.VMEM((2, 4, BATCH * LAGS, 128), jnp.bfloat16),
            pltpu.VMEM((LAGS, BATCH, BAND), jnp.bfloat16),
            pltpu.SemaphoreType.DMA((4,)),
            pltpu.SemaphoreType.DMA((LAGS // CHUNK,)),
        ],
        compiler_params=pltpu.CompilerParams(
            vmem_limit_bytes=VMEM, dimension_semantics=("arbitrary",)
        ),
        cost_estimate=pl.CostEstimate(flops=flops, bytes_accessed=moved_bytes, transcendentals=0),
        name="band_lags",
    )(place, own, *sources, *arrays, table)


def lag_table():
    lag_index = np.arange(LAGS, dtype=np.int64)
    tables = []
    for rank in range(2):
        freq_index = (np.arange(FBINS, dtype=np.int64) + rank * BINS) % FBINS
        angles = (lag_index[:, None] * freq_index[None, :] % NFFT) * (2.0 * math.pi / NFFT)
        values = -np.sin(angles) if rank else np.cos(angles)
        tables.append((values * FBINS ** (-0.5)).astype(np.float32).astype(ml_dtypes.bfloat16))
    return np.stack(tables)


def local(spectra, seg_mask):
    chan = lax.axis_index("chan")
    rank = lax.axis_index("freq")
    core, x, row = chan % 2, chan // 2 % LINE, chan // (2 * LINE) % ROWS
    chips = lax.axis_size("chan") // 2
    place = jnp.stack([core, x, chan // 2, jnp.int32(chips), rank]).astype(jnp.int32)
    edge = jnp.where(rank == 0, spectra[..., BINS - 128 :], spectra[..., :128])
    rim = moved(edge, freq=1)
    own = whiten(rank.astype(jnp.int32).reshape(1), spectra, rim, seg_mask)

    def along(block, j):
        return moved(block, (0, 0, j))

    def flip(block):
        return moved(block, freq=1)

    def swap(block):
        return moved(block, core=1)

    def reached(j):
        return along(jnp.where(x >= j, own, after), j)

    after = moved(own, (1, 0, 0))
    own_flip = flip(own)
    own, after = lax.optimization_barrier((own, after))
    crossing = jnp.where(row == 1, own, after)
    one, three, two = reached(1), reached(3), reached(2)
    cross = moved(crossing, (0, 1, 0))
    cross_flip = moved(crossing, (0, 1, 0), freq=1)
    one, three, two, cross, cross_flip, own_flip = lax.optimization_barrier(
        (one, three, two, cross, cross_flip, own_flip)
    )
    pairs = {0: jnp.stack([cross, cross_flip])}
    row_pair = jnp.stack([one, three])
    row_flip = flip(row_pair)
    pairs[1], pairs[3] = along(pairs[0], 1), along(pairs[0], 3)
    first = [own, own_flip, after]
    early = [swap(jnp.concatenate([jnp.stack(first), pairs[0]])), swap(row_pair)]
    row_flip, pairs[1], pairs[3], own_flip_ = lax.optimization_barrier(
        (row_flip, pairs[1], pairs[3], own_flip)
    )
    two_flip = flip(two)
    cross_two = along(pairs[1][0], 1)
    cross_two_flip = along(pairs[3][1], 3)
    after_flip = moved(own_flip_, (1, 0, 0))
    middle = [row_flip, pairs[1], pairs[3]]
    early.append(swap(jnp.concatenate([*middle, two[None]])))
    late = lax.optimization_barrier((after_flip, two_flip, cross_two, cross_two_flip))
    swapped = [*early, *(swap(block) for block in late)]
    held = [*first, pairs[0], row_pair, *middle, two, *late]
    start = [[(0, 0, 0)], [(0, 0, 1)], [(0, 2, 0)], [(0, 1, 0), (0, 1, 1)]]
    row_names = [[(1, 0, 0), (3, 0, 0)]]
    more = [[(1, 0, 1), (3, 0, 1)], [(1, 1, 0), (1, 1, 1)], [(3, 1, 0), (3, 1, 1)], [(2, 0, 0)]]
    rest = [[(0, 2, 1)], [(2, 0, 1)], [(2, 1, 0)], [(2, 1, 1)]]
    arrays, lies = [], []
    for layer, blocks, names in (
        (0, held, start + row_names + more + rest),
        (1, swapped, [sum(start, []), *row_names, sum(more, [])] + rest),
    ):
        for listed, block in zip(names, blocks):
            arrays.append(block if block.ndim == 4 else block[None])
            lies.append([(*name, layer) for name in listed])
    table = jnp.asarray(lag_table())
    return band_lags(place, own, [own, own_flip], arrays, lies, table)[None]


def solution(mesh):
    placed = (P(None, None, "chan", "freq"), P("chan", None))
    return jax.shard_map(
        local, mesh=mesh, in_specs=placed, out_specs=P("freq", None, "chan", None), check_vma=False
    )
```

```python
import math

import jax
import jax.numpy as jnp
import ml_dtypes
import numpy as np
from jax import lax
from jax.experimental import pallas as pl
from jax.experimental.pallas import tpu as pltpu
from jax.sharding import PartitionSpec as P

BAND = 512
FBINS = 1024
HALF = 64
LAGS = 256
NFFT = 2048
EPSILON = 1e-06
SEGMENTS = 8
CH = 32
BINS = 512
GROUP = 16
GROUPS = BINS // GROUP
DEPTH = 2 * SEGMENTS * GROUP
STEP = 8
UNROLL = 8
BATCH = 16
CHUNK = 16
ROWS = 2
LINE = 4
CSTEP = 8
AXES = ("chan", "freq")
VMEM = 60 * 1024 * 1024
INTERPRET = False


def moved(value, back=(0, 0, 0), core=0, freq=0):
    count, halves = lax.axis_size("chan"), lax.axis_size("freq")
    planes = count // (ROWS * LINE * 2)
    pairs = []
    for index in range(count * halves):
        rest, f = divmod(index, halves)
        rest, k = divmod(rest, 2)
        rest, x = divmod(rest, LINE)
        z, y = divmod(rest, ROWS)
        z, y, x = (z - back[0]) % planes, (y - back[1]) % ROWS, (x - back[2]) % LINE
        pairs.append((index, (((z * ROWS + y) * LINE + x) * 2 + (k ^ core)) * halves + (f ^ freq)))
    return lax.ppermute(value, AXES, pairs)


def whiten_kernel(rank_ref, spectra_ref, rim_ref, mask_ref, out_ref):
    rank = rank_ref[0]
    real = spectra_ref[0].astype(jnp.float32)
    imag = spectra_ref[1].astype(jnp.float32)
    magnitude = jnp.sqrt(real * real + imag * imag).reshape(SEGMENTS * CH, BINS)
    rim_real = rim_ref[0].astype(jnp.float32)
    rim_imag = rim_ref[1].astype(jnp.float32)
    rim = jnp.sqrt(rim_real * rim_real + rim_imag * rim_imag).reshape(SEGMENTS * CH, HALF)

    def window_sum(values, positions):
        target = lax.broadcasted_iota(jnp.int32, (values.shape[1], BINS), 1)
        near = jnp.abs(positions - target) <= HALF
        table = jnp.where(near, 1.0, 0.0).astype(jnp.bfloat16)
        high = values.astype(jnp.bfloat16)
        low = (values - high.astype(jnp.float32)).astype(jnp.bfloat16)
        return jnp.dot(high, table, preferred_element_type=jnp.float32) + jnp.dot(
            low, table, preferred_element_type=jnp.float32
        )

    inner = lax.broadcasted_iota(jnp.int32, (BINS, BINS), 0)
    outer = lax.broadcasted_iota(jnp.int32, (HALF, BINS), 0) + jnp.where(rank == 0, BINS, -HALF)
    summed = window_sum(magnitude, inner) + window_sum(rim, outer)
    bin_index = rank * BINS + lax.broadcasted_iota(jnp.int32, (1, BINS), 1)
    counted = (
        jnp.minimum(bin_index + HALF, FBINS - 1) - jnp.maximum(bin_index - HALF, 0) + 1
    ).astype(jnp.float32)
    levels = summed / counted + EPSILON
    scale = (1.0 / levels).reshape(SEGMENTS, CH, BINS)
    valid = mask_ref[...].astype(jnp.float32)
    out_ref[GROUPS] = jnp.concatenate(
        [valid, jnp.zeros((CH, DEPTH - SEGMENTS), jnp.float32)], 1
    ).astype(jnp.bfloat16)
    lane = lax.broadcasted_iota(jnp.int32, (CH, 128), 1)
    for p, part in enumerate((real, imag)):
        for tile in range(BINS // 128):
            cut = slice(tile * 128, tile * 128 + 128)
            rows = [
                part[s, :, cut] * scale[s, :, cut] * valid[:, s : s + 1] for s in range(SEGMENTS)
            ]
            for bit in (1, 2, 4):
                upper = (lane // GROUP) & bit != 0
                for i in range(SEGMENTS):
                    if i & bit:
                        continue
                    a, b = rows[i], rows[i + bit]
                    rows[i] = jnp.where(upper, pltpu.roll(b, bit * GROUP, 1), a)
                    rows[i + bit] = jnp.where(upper, b, pltpu.roll(a, 128 - bit * GROUP, 1))
            for g in range(SEGMENTS):
                out_ref[tile * SEGMENTS + g, :, p * 128 : p * 128 + 128] = rows[g].astype(
                    jnp.bfloat16
                )


def whiten(rank, spectra, rim, mask):
    return pl.pallas_call(
        whiten_kernel,
        out_shape=jax.ShapeDtypeStruct((GROUPS + 1, CH, DEPTH), jnp.bfloat16),
        in_specs=[pl.BlockSpec(memory_space=pltpu.SMEM)]
        + [pl.BlockSpec(memory_space=pltpu.VMEM)] * 3,
        out_specs=pl.BlockSpec(memory_space=pltpu.VMEM),
        compiler_params=pltpu.CompilerParams(vmem_limit_bytes=VMEM),
        name="whiten",
    )(rank, spectra, rim, mask)


def band_kernel(lies, place_ref, *refs):
    own_ref, source_refs, array_refs = refs[0], refs[1:3], refs[3 : 3 + len(lies)]
    (table_ref, out_ref, rows_ref, flags_ref, diagonal_ref, product_ref, inverse_ref) = refs[
        3 + len(lies) : 10 + len(lies)
    ]
    weights_ref, result_ref, staging_ref, sems, out_sems = refs[10 + len(lies) :]
    core, x, chip, chips, rank = [place_ref[n] for n in range(5)]
    step = pl.program_id(0)
    corr_steps = GROUPS // STEP
    place = {}
    count = 0
    spans = []
    for names in lies:
        spans.append((count, len(names)))
        for name in names:
            place[name] = count
            count += 1

    def order(half):
        listed = []

        def add(kinds, layer):
            listed.append(jnp.where(layer == 0, place[(*kinds, 0)], place[(*kinds, 1)]))

        for j in range(LINE):
            wraps = x + j >= LINE
            for upper in (0, 1):
                for layer in (core, 1 - core):
                    straight = [place[j, upper, half, n] for n in range(2)]
                    turned = [place[j, 1 - upper, half, n] for n in range(2)]
                    listed.append(
                        jnp.where(
                            wraps,
                            jnp.where(layer == 0, turned[0], turned[1]),
                            jnp.where(layer == 0, straight[0], straight[1]),
                        )
                    )
        for layer in (core, 1 - core):
            add((0, 2, half), layer)
        return listed

    def fetch(number):
        slot = number % 2
        for ref, (start, size) in zip(array_refs, spans):
            pltpu.make_async_copy(
                ref.at[:, pl.ds(number * STEP, STEP)],
                rows_ref.at[slot, pl.ds(start, size)],
                sems.at[slot],
            ).start()

    @pl.when(step == 0)
    def begin():
        fetch(0)
        pltpu.make_async_copy(table_ref.at[rank], weights_ref, sems.at[3]).start()
        for ref, (start, size) in zip(array_refs, spans):
            pltpu.make_async_copy(
                ref.at[:, GROUPS], flags_ref.at[pl.ds(start, size)], sems.at[2]
            ).start()

    @pl.when(step < corr_steps)
    def correlate():
        @pl.when(step + 1 < corr_steps)
        def ahead():
            fetch(step + 1)

        slot = step % 2
        pltpu.make_async_copy(rows_ref.at[slot], rows_ref.at[slot], sems.at[slot]).wait()
        lane_bin = lax.broadcasted_iota(jnp.int32, (GROUP, DEPTH), 1) % GROUP
        own_bin = lane_bin == lax.broadcasted_iota(jnp.int32, (GROUP, DEPTH), 0)
        column = lax.broadcasted_iota(jnp.int32, (GROUP, 128), 1)
        orders = [order(half) for half in range(2)]

        def one_group(index, carry):
            for half in range(2):
                source = source_refs[half][index].astype(jnp.float32)
                real, imag = source[:, : DEPTH // 2], source[:, DEPTH // 2 :]
                source = jnp.concatenate(
                    [jnp.where(rank == 0, real, -imag), jnp.where(rank == 0, imag, real)], 1
                )
                for c in range(CH):
                    spread = jnp.broadcast_to(source[c : c + 1, :], (GROUP, DEPTH))
                    diagonal_ref[half, c * GROUP : (c + 1) * GROUP, :] = jnp.where(
                        own_bin, spread, 0.0
                    ).astype(jnp.bfloat16)
                rows = jnp.concatenate([rows_ref[slot, at, index] for at in orders[half]], 0)
                product = lax.dot_general(
                    diagonal_ref[half],
                    rows,
                    (((1,), (1,)), ((), ())),
                    preferred_element_type=jnp.float32,
                )
                first_bin = pl.multiple_of(half * BINS + (step * STEP + index) * GROUP, GROUP)
                for c in range(CH):
                    part = product[c * GROUP : (c + 1) * GROUP]
                    here = pl.ds(c * FBINS + first_bin, GROUP)
                    tail = jnp.concatenate([part[:, BAND:], part[:, 64:128]], 1)
                    head = jnp.where(column >= 32 * core + c, part[:, :128], tail)
                    product_ref[here, :] = jnp.concatenate([head, part[:, 128:BAND]], 1).astype(
                        jnp.bfloat16
                    )
            return carry

        lax.fori_loop(0, STEP, one_group, 0, unroll=UNROLL)

    @pl.when(step == corr_steps)
    def scales():
        pltpu.make_async_copy(table_ref.at[rank], weights_ref, sems.at[3]).wait()
        pltpu.make_async_copy(flags_ref, flags_ref, sems.at[2]).wait()
        counts = lax.dot_general(
            own_ref[0],
            jnp.concatenate([flags_ref[at] for at in order(0)], 0),
            (((1,), (1,)), ((), ())),
            preferred_element_type=jnp.float32,
        )
        inverse = 1.0 / jnp.maximum(counts, 1.0)
        column = lax.broadcasted_iota(jnp.int32, (CH, 64), 1)
        channel = lax.broadcasted_iota(jnp.int32, (CH, 64), 0)
        parts = []
        for n in range(8):
            offset = n // 2 + 4 * (n % 2)
            part = jnp.where(chip + offset < chips, inverse[:, 64 * n : 64 * n + 64], 0.0)
            if offset == 0:
                after = jnp.where(chip + 8 < chips, inverse[:, BAND:], 0.0)
                part = jnp.where(column >= 32 * core + channel, part, after)
            parts.append(part)
        whole = jnp.concatenate(parts, 1)
        for c in range(CH):
            inverse_ref[c] = whole[c : c + 1]

    def one_channel(c):
        lags = jnp.dot(
            weights_ref[...],
            product_ref[pl.ds(pl.multiple_of(c * FBINS, FBINS), FBINS), :],
            preferred_element_type=jnp.float32,
        )
        lags = (lags * inverse_ref[c]).astype(jnp.bfloat16)
        tiles = [lags[:, 128 * j : 128 * j + 128] for j in range(LINE)]
        shift = 32 * core + c
        low = [pltpu.roll(tile, (128 - shift) % 128, 1) for tile in tiles]
        high = [pltpu.roll(tile, 64 - shift, 1) for tile in tiles]
        lane = lax.broadcasted_iota(jnp.int32, (LAGS, 128), 1)
        first, second = lane < 64 - shift, lane < 128 - shift
        rows = pl.ds(pl.multiple_of(c % BATCH * LAGS, LAGS), LAGS)
        for u, (one, two, three) in enumerate(
            (
                (low[0], high[1], low[2]),
                (low[2], high[3], high[0]),
                (high[0], low[1], high[2]),
                (high[2], low[3], low[0]),
            )
        ):
            result_ref[c // BATCH, u, rows, :] = jnp.where(first, one, jnp.where(second, two, three))

    def flush(batch, chunk):
        at = pl.multiple_of(chunk * CHUNK, CHUNK)
        for u in range(4):
            block = jnp.stack(
                [result_ref[batch, u, pl.ds(n * LAGS + at, CHUNK), :] for n in range(BATCH)]
            ).astype(jnp.float32)
            staging_ref[pl.ds(at, CHUNK), :, u * 128 : u * 128 + 128] = jnp.swapaxes(
                block, 0, 1
            ).astype(jnp.bfloat16)

    def leaving(batch, chunk):
        at = pl.multiple_of(chunk * CHUNK, CHUNK)
        return pltpu.make_async_copy(
            staging_ref.at[pl.ds(at, CHUNK)],
            out_ref.at[pl.ds(at, CHUNK), pl.ds(batch * BATCH, BATCH), :],
            out_sems.at[chunk],
        )

    lag_step = step - corr_steps
    batch_steps = BATCH // CSTEP

    @pl.when(jnp.logical_and(step >= corr_steps, lag_step < batch_steps))
    def first_batch():
        lax.fori_loop(0, CSTEP, lambda n, carry: one_channel(lag_step * CSTEP + n), None, unroll=CSTEP)

    @pl.when(lag_step >= batch_steps)
    def second_batch():
        def one(n, carry):
            c = lag_step * CSTEP + n
            one_channel(c)
            flush(0, c - BATCH)
            leaving(0, c - BATCH).start()

        lax.fori_loop(0, CSTEP, one, None, unroll=CSTEP)

    @pl.when(lag_step == 2 * batch_steps - 1)
    def last_flush():
        def one(n, carry):
            leaving(0, n).wait()
            flush(1, n)
            leaving(1, n).start()

        lax.fori_loop(0, LAGS // CHUNK, one, None, unroll=2)
        lax.fori_loop(0, LAGS // CHUNK, lambda n, carry: leaving(1, n).wait(), None)


def band_lags(place, own, sources, arrays, lies, table):
    corr_steps = GROUPS // STEP
    blocks = sum(map(len, lies))
    source_spec = pl.BlockSpec((STEP, CH, DEPTH), lambda i: (jnp.minimum(i, corr_steps - 1), 0, 0))
    flops = 2 * CH * FBINS * BAND * (DEPTH + LAGS)
    moved_bytes = 2 * blocks * CH * DEPTH * GROUPS + 2 * CH * LAGS * BAND
    return pl.pallas_call(
        lambda *refs: band_kernel(lies, *refs),
        grid=(corr_steps + CH // CSTEP,),
        out_shape=jax.ShapeDtypeStruct((LAGS, CH, BAND), jnp.bfloat16),
        in_specs=[
            pl.BlockSpec(memory_space=pltpu.SMEM),
            pl.BlockSpec((1, CH, DEPTH), lambda i: (GROUPS, 0, 0)),
            source_spec,
            source_spec,
        ]
        + [pl.BlockSpec(memory_space=pl.ANY)] * (len(arrays) + 1),
        out_specs=pl.BlockSpec(memory_space=pl.ANY),
        scratch_shapes=[
            pltpu.VMEM((2, blocks, STEP, CH, DEPTH), jnp.bfloat16),
            pltpu.VMEM((blocks, CH, DEPTH), jnp.bfloat16),
            pltpu.VMEM((2, CH * GROUP, DEPTH), jnp.bfloat16),
            pltpu.VMEM((CH * FBINS, BAND), jnp.bfloat16),
            pltpu.VMEM((CH, 1, BAND), jnp.float32),
            pltpu.VMEM((LAGS, FBINS), jnp.bfloat16),
            pltpu.VMEM((2, 4, BATCH * LAGS, 128), jnp.bfloat16),
            pltpu.VMEM((LAGS, BATCH, BAND), jnp.bfloat16),
            pltpu.SemaphoreType.DMA((4,)),
            pltpu.SemaphoreType.DMA((LAGS // CHUNK,)),
        ],
        compiler_params=pltpu.CompilerParams(
            vmem_limit_bytes=VMEM, dimension_semantics=("arbitrary",)
        ),
        cost_estimate=pl.CostEstimate(flops=flops, bytes_accessed=moved_bytes, transcendentals=0),
        name="band_lags",
    )(place, own, *sources, *arrays, table)


def lag_table():
    lag_index = np.arange(LAGS, dtype=np.int64)
    tables = []
    for rank in range(2):
        freq_index = (np.arange(FBINS, dtype=np.int64) + rank * BINS) % FBINS
        angles = (lag_index[:, None] * freq_index[None, :] % NFFT) * (2.0 * math.pi / NFFT)
        values = -np.sin(angles) if rank else np.cos(angles)
        tables.append((values * FBINS ** (-0.5)).astype(np.float32).astype(ml_dtypes.bfloat16))
    return np.stack(tables)


def local(spectra, seg_mask):
    chan = lax.axis_index("chan")
    rank = lax.axis_index("freq")
    core, x, row = chan % 2, chan // 2 % LINE, chan // (2 * LINE) % ROWS
    chips = lax.axis_size("chan") // 2
    place = jnp.stack([core, x, chan // 2, jnp.int32(chips), rank]).astype(jnp.int32)
    edge = jnp.where(rank == 0, spectra[..., BINS - HALF :], spectra[..., :HALF])
    rim = moved(edge, freq=1)
    own = whiten(rank.astype(jnp.int32).reshape(1), spectra, rim, seg_mask)

    def along(block, j):
        return moved(block, (0, 0, j))

    def flip(block):
        return moved(block, freq=1)

    def swap(block):
        return moved(block, core=1)

    def reached(j):
        return along(jnp.where(x >= j, own, after), j)

    after = moved(own, (1, 0, 0))
    own_flip = flip(own)
    own, after = lax.optimization_barrier((own, after))
    crossing = jnp.where(row == 1, own, after)
    one, three = reached(1), reached(3)
    cross = moved(crossing, (0, 1, 0))
    cross_flip = moved(crossing, (0, 1, 0), freq=1)
    one, three, cross, cross_flip, own_flip = lax.optimization_barrier(
        (one, three, cross, cross_flip, own_flip)
    )
    pairs = {0: jnp.stack([cross, cross_flip])}
    row_pair = jnp.stack([one, three])
    row_flip = flip(row_pair)
    pairs[1], pairs[3] = along(pairs[0], 1), along(pairs[0], 3)
    two = reached(2)
    after_flip = moved(own_flip, (1, 0, 0))
    row_flip, after_flip, *gated = lax.optimization_barrier(
        (row_flip, after_flip, own, own_flip, after, pairs[0], row_pair)
    )
    swapped = [
        swap(jnp.stack([*gated[:3], after_flip])),
        swap(jnp.concatenate([*gated[3:], row_flip])),
    ]
    pairs[1], pairs[3], two = lax.optimization_barrier((pairs[1], pairs[3], two))
    two_flip = flip(two)
    cross_two = along(pairs[1][0], 1)
    cross_two_flip = along(pairs[3][1], 3)
    late = lax.optimization_barrier(
        (pairs[1], pairs[3], two, two_flip, cross_two, cross_two_flip)
    )
    swapped += [swap(block) for block in late]
    held = [own, own_flip, after, after_flip, pairs[0], row_pair, row_flip, *late]
    one_by_one = [[(0, 0, 0)], [(0, 0, 1)], [(0, 2, 0)], [(0, 2, 1)]]
    in_pairs = [[(0, 1, 0), (0, 1, 1)], [(1, 0, 0), (3, 0, 0)], [(1, 0, 1), (3, 0, 1)]]
    rest = [[(1, 1, 0), (1, 1, 1)], [(3, 1, 0), (3, 1, 1)]]
    rest += [[(2, 0, 0)], [(2, 0, 1)], [(2, 1, 0)], [(2, 1, 1)]]
    arrays, lies = [], []
    for layer, blocks, names in (
        (0, held, one_by_one + in_pairs + rest),
        (1, swapped, [sum(one_by_one, []), sum(in_pairs, [])] + rest),
    ):
        for listed, block in zip(names, blocks):
            arrays.append(block if block.ndim == 4 else block[None])
            lies.append([(*name, layer) for name in listed])
    table = jnp.asarray(lag_table())
    return band_lags(place, own, [own, own_flip], arrays, lies, table)[None]


def solution(mesh):
    placed = (P(None, None, "chan", "freq"), P("chan", None))
    return jax.shard_map(
        local, mesh=mesh, in_specs=placed, out_specs=P("freq", None, "chan", None), check_vma=False
    )
```

```python
import math

import jax
import jax.numpy as jnp
import ml_dtypes
import numpy as np
from jax import lax
from jax.experimental import pallas as pl
from jax.experimental.pallas import tpu as pltpu
from jax.sharding import PartitionSpec as P

BAND = 512
FBINS = 1024
HALF = 64
LAGS = 256
NFFT = 2048
EPSILON = 1e-06
SEGMENTS = 8
CH = 32
BINS = 512
GROUP = 16
GROUPS = BINS // GROUP
DEPTH = 2 * SEGMENTS * GROUP
STEP = 8
UNROLL = 8
BATCH = 16
CHUNK = 16
ROWS = 2
LINE = 4
CSTEP = 8
AXES = ("chan", "freq")
VMEM = 60 * 1024 * 1024
INTERPRET = False


def moved(value, back=(0, 0, 0), core=0, freq=0):
    count, halves = lax.axis_size("chan"), lax.axis_size("freq")
    planes = count // (ROWS * LINE * 2)
    pairs = []
    for index in range(count * halves):
        rest, f = divmod(index, halves)
        rest, k = divmod(rest, 2)
        rest, x = divmod(rest, LINE)
        z, y = divmod(rest, ROWS)
        z, y, x = (z - back[0]) % planes, (y - back[1]) % ROWS, (x - back[2]) % LINE
        pairs.append((index, (((z * ROWS + y) * LINE + x) * 2 + (k ^ core)) * halves + (f ^ freq)))
    return lax.ppermute(value, AXES, pairs)


def whiten_kernel(rank_ref, spectra_ref, rim_ref, mask_ref, out_ref):
    rank = rank_ref[0]
    real = spectra_ref[0].astype(jnp.float32)
    imag = spectra_ref[1].astype(jnp.float32)
    magnitude = jnp.sqrt(real * real + imag * imag).reshape(SEGMENTS * CH, BINS)
    rim_real = rim_ref[0].astype(jnp.float32)
    rim_imag = rim_ref[1].astype(jnp.float32)
    rim = jnp.sqrt(rim_real * rim_real + rim_imag * rim_imag).reshape(SEGMENTS * CH, HALF)

    def window_sum(values, positions):
        target = lax.broadcasted_iota(jnp.int32, (values.shape[1], BINS), 1)
        near = jnp.abs(positions - target) <= HALF
        table = jnp.where(near, 1.0, 0.0).astype(jnp.bfloat16)
        high = values.astype(jnp.bfloat16)
        low = (values - high.astype(jnp.float32)).astype(jnp.bfloat16)
        return jnp.dot(high, table, preferred_element_type=jnp.float32) + jnp.dot(
            low, table, preferred_element_type=jnp.float32
        )

    inner = lax.broadcasted_iota(jnp.int32, (BINS, BINS), 0)
    outer = lax.broadcasted_iota(jnp.int32, (HALF, BINS), 0) + jnp.where(rank == 0, BINS, -HALF)
    summed = window_sum(magnitude, inner) + window_sum(rim, outer)
    bin_index = rank * BINS + lax.broadcasted_iota(jnp.int32, (1, BINS), 1)
    counted = (
        jnp.minimum(bin_index + HALF, FBINS - 1) - jnp.maximum(bin_index - HALF, 0) + 1
    ).astype(jnp.float32)
    levels = summed / counted + EPSILON
    scale = (1.0 / levels).reshape(SEGMENTS, CH, BINS)
    valid = mask_ref[...].astype(jnp.float32)
    out_ref[GROUPS] = jnp.concatenate(
        [valid, jnp.zeros((CH, DEPTH - SEGMENTS), jnp.float32)], 1
    ).astype(jnp.bfloat16)
    lane = lax.broadcasted_iota(jnp.int32, (CH, 128), 1)
    for p, part in enumerate((real, imag)):
        for tile in range(BINS // 128):
            cut = slice(tile * 128, tile * 128 + 128)
            rows = [
                part[s, :, cut] * scale[s, :, cut] * valid[:, s : s + 1] for s in range(SEGMENTS)
            ]
            for bit in (1, 2, 4):
                upper = (lane // GROUP) & bit != 0
                for i in range(SEGMENTS):
                    if i & bit:
                        continue
                    a, b = rows[i], rows[i + bit]
                    rows[i] = jnp.where(upper, pltpu.roll(b, bit * GROUP, 1), a)
                    rows[i + bit] = jnp.where(upper, b, pltpu.roll(a, 128 - bit * GROUP, 1))
            for g in range(SEGMENTS):
                out_ref[tile * SEGMENTS + g, :, p * 128 : p * 128 + 128] = rows[g].astype(
                    jnp.bfloat16
                )


def whiten(rank, spectra, rim, mask):
    return pl.pallas_call(
        whiten_kernel,
        out_shape=jax.ShapeDtypeStruct((GROUPS + 1, CH, DEPTH), jnp.bfloat16),
        in_specs=[pl.BlockSpec(memory_space=pltpu.SMEM)]
        + [pl.BlockSpec(memory_space=pltpu.VMEM)] * 3,
        out_specs=pl.BlockSpec(memory_space=pltpu.VMEM),
        compiler_params=pltpu.CompilerParams(vmem_limit_bytes=VMEM),
        name="whiten",
    )(rank, spectra, rim, mask)


def band_kernel(lies, place_ref, *refs):
    own_ref, source_refs, array_refs = refs[0], refs[1:3], refs[3 : 3 + len(lies)]
    (table_ref, out_ref, rows_ref, flags_ref, diagonal_ref, product_ref, inverse_ref) = refs[
        3 + len(lies) : 10 + len(lies)
    ]
    weights_ref, result_ref, staging_ref, sems, out_sems = refs[10 + len(lies) :]
    core, x, chip, chips, rank = [place_ref[n] for n in range(5)]
    step = pl.program_id(0)
    corr_steps = GROUPS // STEP
    place = {}
    count = 0
    spans = []
    for names in lies:
        spans.append((count, len(names)))
        for name in names:
            place[name] = count
            count += 1

    def order(half):
        listed = []

        def add(kinds, layer):
            listed.append(jnp.where(layer == 0, place[(*kinds, 0)], place[(*kinds, 1)]))

        for j in range(LINE):
            wraps = x + j >= LINE
            for upper in (0, 1):
                for layer in (core, 1 - core):
                    straight = [place[j, upper, half, n] for n in range(2)]
                    turned = [place[j, 1 - upper, half, n] for n in range(2)]
                    listed.append(
                        jnp.where(
                            wraps,
                            jnp.where(layer == 0, turned[0], turned[1]),
                            jnp.where(layer == 0, straight[0], straight[1]),
                        )
                    )
        for layer in (core, 1 - core):
            add((0, 2, half), layer)
        return listed

    def fetch(number):
        slot = number % 2
        for ref, (start, size) in zip(array_refs, spans):
            pltpu.make_async_copy(
                ref.at[:, pl.ds(number * STEP, STEP)],
                rows_ref.at[slot, pl.ds(start, size)],
                sems.at[slot],
            ).start()

    @pl.when(step == 0)
    def begin():
        fetch(0)
        pltpu.make_async_copy(table_ref.at[rank], weights_ref, sems.at[3]).start()
        for ref, (start, size) in zip(array_refs, spans):
            pltpu.make_async_copy(
                ref.at[:, GROUPS], flags_ref.at[pl.ds(start, size)], sems.at[2]
            ).start()

    @pl.when(step < corr_steps)
    def correlate():
        @pl.when(step + 1 < corr_steps)
        def ahead():
            fetch(step + 1)

        slot = step % 2
        pltpu.make_async_copy(rows_ref.at[slot], rows_ref.at[slot], sems.at[slot]).wait()
        lane_bin = lax.broadcasted_iota(jnp.int32, (GROUP, DEPTH), 1) % GROUP
        own_bin = lane_bin == lax.broadcasted_iota(jnp.int32, (GROUP, DEPTH), 0)
        column = lax.broadcasted_iota(jnp.int32, (GROUP, 128), 1)
        orders = [order(half) for half in range(2)]

        def one_group(index, carry):
            for half in range(2):
                source = source_refs[half][index].astype(jnp.float32)
                real, imag = source[:, : DEPTH // 2], source[:, DEPTH // 2 :]
                source = jnp.concatenate(
                    [jnp.where(rank == 0, real, -imag), jnp.where(rank == 0, imag, real)], 1
                )
                for c in range(CH):
                    spread = jnp.broadcast_to(source[c : c + 1, :], (GROUP, DEPTH))
                    diagonal_ref[half, c * GROUP : (c + 1) * GROUP, :] = jnp.where(
                        own_bin, spread, 0.0
                    ).astype(jnp.bfloat16)
                rows = jnp.concatenate([rows_ref[slot, at, index] for at in orders[half]], 0)
                product = lax.dot_general(
                    diagonal_ref[half],
                    rows,
                    (((1,), (1,)), ((), ())),
                    preferred_element_type=jnp.float32,
                )
                first_bin = pl.multiple_of(half * BINS + (step * STEP + index) * GROUP, GROUP)
                for c in range(CH):
                    part = product[c * GROUP : (c + 1) * GROUP]
                    here = pl.ds(c * FBINS + first_bin, GROUP)
                    tail = jnp.concatenate([part[:, BAND:], part[:, 64:128]], 1)
                    head = jnp.where(column >= 32 * core + c, part[:, :128], tail)
                    product_ref[here, :] = jnp.concatenate([head, part[:, 128:BAND]], 1).astype(
                        jnp.bfloat16
                    )
            return carry

        lax.fori_loop(0, STEP, one_group, 0, unroll=UNROLL)

    @pl.when(step == corr_steps)
    def scales():
        pltpu.make_async_copy(table_ref.at[rank], weights_ref, sems.at[3]).wait()
        pltpu.make_async_copy(flags_ref, flags_ref, sems.at[2]).wait()
        counts = lax.dot_general(
            own_ref[0],
            jnp.concatenate([flags_ref[at] for at in order(0)], 0),
            (((1,), (1,)), ((), ())),
            preferred_element_type=jnp.float32,
        )
        inverse = 1.0 / jnp.maximum(counts, 1.0)
        column = lax.broadcasted_iota(jnp.int32, (CH, 64), 1)
        channel = lax.broadcasted_iota(jnp.int32, (CH, 64), 0)
        parts = []
        for n in range(8):
            offset = n // 2 + 4 * (n % 2)
            part = jnp.where(chip + offset < chips, inverse[:, 64 * n : 64 * n + 64], 0.0)
            if offset == 0:
                after = jnp.where(chip + 8 < chips, inverse[:, BAND:], 0.0)
                part = jnp.where(column >= 32 * core + channel, part, after)
            parts.append(part)
        whole = jnp.concatenate(parts, 1)
        for c in range(CH):
            inverse_ref[c] = whole[c : c + 1]

    def one_channel(c):
        lags = jnp.dot(
            weights_ref[...],
            product_ref[pl.ds(pl.multiple_of(c * FBINS, FBINS), FBINS), :],
            preferred_element_type=jnp.float32,
        )
        lags = (lags * inverse_ref[c]).astype(jnp.bfloat16)
        tiles = [lags[:, 128 * j : 128 * j + 128] for j in range(LINE)]
        shift = 32 * core + c
        low = [pltpu.roll(tile, (128 - shift) % 128, 1) for tile in tiles]
        high = [pltpu.roll(tile, 64 - shift, 1) for tile in tiles]
        lane = lax.broadcasted_iota(jnp.int32, (LAGS, 128), 1)
        first, second = lane < 64 - shift, lane < 128 - shift
        rows = pl.ds(pl.multiple_of(c % BATCH * LAGS, LAGS), LAGS)
        for u, (one, two, three) in enumerate(
            (
                (low[0], high[1], low[2]),
                (low[2], high[3], high[0]),
                (high[0], low[1], high[2]),
                (high[2], low[3], low[0]),
            )
        ):
            result_ref[c // BATCH, u, rows, :] = jnp.where(first, one, jnp.where(second, two, three))

    def flush(batch, chunk):
        at = pl.multiple_of(chunk * CHUNK, CHUNK)
        for u in range(4):
            block = jnp.stack(
                [result_ref[batch, u, pl.ds(n * LAGS + at, CHUNK), :] for n in range(BATCH)]
            ).astype(jnp.float32)
            staging_ref[pl.ds(at, CHUNK), :, u * 128 : u * 128 + 128] = jnp.swapaxes(
                block, 0, 1
            ).astype(jnp.bfloat16)

    def leaving(batch, chunk):
        at = pl.multiple_of(chunk * CHUNK, CHUNK)
        return pltpu.make_async_copy(
            staging_ref.at[pl.ds(at, CHUNK)],
            out_ref.at[pl.ds(at, CHUNK), pl.ds(batch * BATCH, BATCH), :],
            out_sems.at[chunk],
        )

    lag_step = step - corr_steps
    batch_steps = BATCH // CSTEP

    @pl.when(jnp.logical_and(step >= corr_steps, lag_step < batch_steps))
    def first_batch():
        lax.fori_loop(0, CSTEP, lambda n, carry: one_channel(lag_step * CSTEP + n), None, unroll=CSTEP)

    @pl.when(lag_step >= batch_steps)
    def second_batch():
        def one(n, carry):
            c = lag_step * CSTEP + n
            one_channel(c)
            flush(0, c - BATCH)
            leaving(0, c - BATCH).start()

        lax.fori_loop(0, CSTEP, one, None, unroll=CSTEP)

    @pl.when(lag_step == 2 * batch_steps - 1)
    def last_flush():
        def one(n, carry):
            leaving(0, n).wait()
            flush(1, n)
            leaving(1, n).start()

        lax.fori_loop(0, LAGS // CHUNK, one, None, unroll=2)
        lax.fori_loop(0, LAGS // CHUNK, lambda n, carry: leaving(1, n).wait(), None)


def band_lags(place, own, sources, arrays, lies, table):
    corr_steps = GROUPS // STEP
    blocks = sum(map(len, lies))
    source_spec = pl.BlockSpec((STEP, CH, DEPTH), lambda i: (jnp.minimum(i, corr_steps - 1), 0, 0))
    flops = 2 * CH * FBINS * BAND * (DEPTH + LAGS)
    moved_bytes = 2 * blocks * CH * DEPTH * GROUPS + 2 * CH * LAGS * BAND
    return pl.pallas_call(
        lambda *refs: band_kernel(lies, *refs),
        grid=(corr_steps + CH // CSTEP,),
        out_shape=jax.ShapeDtypeStruct((LAGS, CH, BAND), jnp.bfloat16),
        in_specs=[
            pl.BlockSpec(memory_space=pltpu.SMEM),
            pl.BlockSpec((1, CH, DEPTH), lambda i: (GROUPS, 0, 0)),
            source_spec,
            source_spec,
        ]
        + [pl.BlockSpec(memory_space=pl.ANY)] * (len(arrays) + 1),
        out_specs=pl.BlockSpec(memory_space=pl.ANY),
        scratch_shapes=[
            pltpu.VMEM((2, blocks, STEP, CH, DEPTH), jnp.bfloat16),
            pltpu.VMEM((blocks, CH, DEPTH), jnp.bfloat16),
            pltpu.VMEM((2, CH * GROUP, DEPTH), jnp.bfloat16),
            pltpu.VMEM((CH * FBINS, BAND), jnp.bfloat16),
            pltpu.VMEM((CH, 1, BAND), jnp.float32),
            pltpu.VMEM((LAGS, FBINS), jnp.bfloat16),
            pltpu.VMEM((2, 4, BATCH * LAGS, 128), jnp.bfloat16),
            pltpu.VMEM((LAGS, BATCH, BAND), jnp.bfloat16),
            pltpu.SemaphoreType.DMA((4,)),
            pltpu.SemaphoreType.DMA((LAGS // CHUNK,)),
        ],
        compiler_params=pltpu.CompilerParams(
            vmem_limit_bytes=VMEM, dimension_semantics=("arbitrary",)
        ),
        cost_estimate=pl.CostEstimate(flops=flops, bytes_accessed=moved_bytes, transcendentals=0),
        name="band_lags",
    )(place, own, *sources, *arrays, table)


def lag_table():
    lag_index = np.arange(LAGS, dtype=np.int64)
    tables = []
    for rank in range(2):
        freq_index = (np.arange(FBINS, dtype=np.int64) + rank * BINS) % FBINS
        angles = (lag_index[:, None] * freq_index[None, :] % NFFT) * (2.0 * math.pi / NFFT)
        values = -np.sin(angles) if rank else np.cos(angles)
        tables.append((values * FBINS ** (-0.5)).astype(np.float32).astype(ml_dtypes.bfloat16))
    return np.stack(tables)


def local(spectra, seg_mask):
    chan = lax.axis_index("chan")
    rank = lax.axis_index("freq")
    core, x, row = chan % 2, chan // 2 % LINE, chan // (2 * LINE) % ROWS
    chips = lax.axis_size("chan") // 2
    place = jnp.stack([core, x, chan // 2, jnp.int32(chips), rank]).astype(jnp.int32)
    edge = jnp.where(rank == 0, spectra[..., BINS - HALF :], spectra[..., :HALF])
    rim = moved(edge, freq=1)
    own = whiten(rank.astype(jnp.int32).reshape(1), spectra, rim, seg_mask)

    def along(block, j):
        return moved(block, (0, 0, j))

    def flip(block):
        return moved(block, freq=1)

    def swap(block):
        return moved(block, core=1)

    def reached(j):
        return along(jnp.where(x >= j, own, after), j)

    after = moved(own, (1, 0, 0))
    own_flip = flip(own)
    own, after = lax.optimization_barrier((own, after))
    crossing = jnp.where(row == 1, own, after)
    one, three, two = reached(1), reached(3), reached(2)
    cross = moved(crossing, (0, 1, 0))
    cross_flip = moved(crossing, (0, 1, 0), freq=1)
    one, three, two, cross, cross_flip, own_flip = lax.optimization_barrier(
        (one, three, two, cross, cross_flip, own_flip)
    )
    pairs = {0: jnp.stack([cross, cross_flip])}
    row_pair = jnp.stack([one, three])
    row_flip = flip(row_pair)
    pairs[1], pairs[3] = along(pairs[0], 1), along(pairs[0], 3)
    after_flip = moved(own_flip, (1, 0, 0))
    row_flip, after_flip, *gated = lax.optimization_barrier(
        (row_flip, after_flip, own, own_flip, after, pairs[0], row_pair)
    )
    swapped = [
        swap(jnp.stack([*gated[:3], after_flip])),
        swap(jnp.concatenate([*gated[3:], row_flip])),
    ]
    pairs[1], pairs[3] = lax.optimization_barrier((pairs[1], pairs[3]))
    two_flip = flip(two)
    cross_two = along(pairs[1][0], 1)
    cross_two_flip = along(pairs[3][1], 3)
    late = lax.optimization_barrier(
        (pairs[1], pairs[3], two, two_flip, cross_two, cross_two_flip)
    )
    swapped += [swap(block) for block in late]
    held = [own, own_flip, after, after_flip, pairs[0], row_pair, row_flip, *late]
    one_by_one = [[(0, 0, 0)], [(0, 0, 1)], [(0, 2, 0)], [(0, 2, 1)]]
    in_pairs = [[(0, 1, 0), (0, 1, 1)], [(1, 0, 0), (3, 0, 0)], [(1, 0, 1), (3, 0, 1)]]
    rest = [[(1, 1, 0), (1, 1, 1)], [(3, 1, 0), (3, 1, 1)]]
    rest += [[(2, 0, 0)], [(2, 0, 1)], [(2, 1, 0)], [(2, 1, 1)]]
    arrays, lies = [], []
    for layer, blocks, names in (
        (0, held, one_by_one + in_pairs + rest),
        (1, swapped, [sum(one_by_one, []), sum(in_pairs, [])] + rest),
    ):
        for listed, block in zip(names, blocks):
            arrays.append(block if block.ndim == 4 else block[None])
            lies.append([(*name, layer) for name in listed])
    table = jnp.asarray(lag_table())
    return band_lags(place, own, [own, own_flip], arrays, lies, table)[None]


def solution(mesh):
    placed = (P(None, None, "chan", "freq"), P("chan", None))
    return jax.shard_map(
        local, mesh=mesh, in_specs=placed, out_specs=P("freq", None, "chan", None), check_vma=False
    )
```
